128 devices in a mesh: row: 8 (over y, core), col: 16 (over z, x).
Axes of the slice: x: 4, y: 4, z: 4, core: 2. Of those that a mesh axis runs over, the one named last changes fastest.
Arguments:
- parent_blocks: float32 [8, 2048, 2048], P('row', 'col'), as said below
- shifts: float32 [8], replicated, may hold values from -0.5 to 0.5
- orders: int32 [8], replicated, may hold values from 256 to 2048, as said below
- child_order: int32 [8], replicated, may hold values from 0 to 7, each once
Outputs:
- polar: float32 [8, 2048, 2048], P('row', 'col')
The draws below stay inside these ranges and needn't reach their ends.
Inputs may be any that keep to these rules, and one draw needn't show every extreme that they name: `orders`: each order is a multiple of 128 from 256 to 2048; some subproblem has order 2048. `parent_blocks`: each matrix is symmetric. `child_order`: a permutation of the subproblems; slot k lies in child group k.
All inputs are finite; a program needn't handle non-finite values.
Results may differ from the reference program's by a relative error of at most 0.0001.
Values sent between devices are 32-bit elements; how exact they have to be, the bound alone decides.
A program may use at most 64 MiB of HBM per device.

```python
import jax
import jax.numpy as jnp
from jax import lax

M = 2048
STEPS = 2
SUBS = 8
GRAIN = 128


def draw_parent_blocks(key, part):
    key = jax.random.fold_in(key, 1)
    base = jax.random.normal(key, (SUBS, M, M), jnp.float32)
    return (base + jnp.swapaxes(base, 1, 2)) * (0.70710678 / M ** 0.5)


def draw_orders(key, part):
    key = jax.random.fold_in(key, 2)
    first, second = jax.random.split(key)
    values = jax.random.randint(first, (SUBS,), 2, 17) * GRAIN
    where_full = jax.random.randint(second, (), 0, SUBS)
    return values.at[where_full].set(M).astype(jnp.int32)


def setup_inputs(seed: int = 0) -> dict:
    key_list = jax.random.split(jax.random.key(seed), 5)
    parent_blocks = draw_parent_blocks(jax.random.fold_in(key_list[4], 71), 0)
    shifts = jnp.clip(jax.random.uniform(key_list[1], (SUBS,), jnp.float32, -0.5, 0.5), -0.5, 0.5)
    orders = draw_orders(jax.random.fold_in(key_list[4], 71), 0)
    child_order = jax.random.permutation(key_list[3], SUBS).astype(jnp.int32)
    return {"parent_blocks": parent_blocks, "shifts": shifts, "orders": orders, "child_order": child_order}


def matmul_batch(left, right):
    return jnp.einsum('sik,skj->sij', left, right, precision=lax.Precision.HIGHEST)

def reference(parent_blocks, shifts, orders, child_order):
    index_all = jnp.arange(M, dtype=jnp.int32)
    limit = orders[:, None, None]
    live = (index_all[None, :, None] < limit) & (index_all[None, None, :] < limit)
    diagonal = index_all[:, None] == index_all[None, :]
    moved = parent_blocks - jnp.where(diagonal[None], shifts[:, None, None], jnp.float32(0.0))
    shifted = jnp.where(live, moved, jnp.float32(0.0))
    sumsq = lax.optimization_barrier(jnp.sum(shifted * shifted, axis=(1, 2)))
    root_order = jnp.sqrt(orders.astype(jnp.float32))
    scale = root_order / (2.0 * jnp.sqrt(sumsq + 1e-06))
    iterate = shifted * scale[:, None, None]
    for step in range(STEPS):
        square = matmul_batch(iterate, iterate)
        cubic = matmul_batch(iterate, square)
        iterate = 1.5 * iterate - 0.5 * cubic
    result = iterate * root_order[:, None, None]
    return result[child_order]
```

```python
import jax
import jax.numpy as jnp
from jax import lax
from jax.experimental import pallas as pl
from jax.experimental.pallas import tpu as pltpu
from jax.sharding import PartitionSpec as P

MESH = pl.DeviceIdType.MESH
f32, bf16 = jnp.float32, jnp.bfloat16

SIDE = 4
STRIPS = SIDE * SIDE
ROWS = 8
B = 128
M = STRIPS * B
TILE = 1024

HALVES = ((0, 2), (2, 0), (2, 2))
CHUNKS = (
    ("x", ((0, 0), (0, 1))),
    ("z", ((2, 1),) + HALVES),
    ("x", ((1, 0), (1, 1))),
    ("z", ((1, 2), (1, 3))),
)
LINE = {"x": (0, 1), "z": (1, 0)}


def block_rows(d):
    return B // 2 if d in HALVES else B


def chunk_rows(q):
    return sum(block_rows(d) for d in CHUNKS[q][1])


def offset(q, d):
    total = 0
    for e in CHUNKS[q][1]:
        if e == d:
            return total
        total += block_rows(e)


def plus(r, e, k=1):
    return ((r[0] + k * e[0]) % SIDE, (r[1] + k * e[1]) % SIDE)


def flat(r):
    return SIDE * r[0] + r[1]


def split(v):
    high = v.astype(bf16)
    return high, (v - high.astype(f32)).astype(bf16)


def kernel(x_ref, shifts, orders, child, o_ref, *scratch):
    nq = len(CHUNKS)
    pack, parts, chosen, stage = (scratch[i * nq : (i + 1) * nq] for i in range(4))
    sh, sl, lhs, cur, first_strip, res, ssq, scale, s1, r1, s2, r2, s3, r3 = scratch[4 * nq :]

    row, col = lax.axis_index("row"), lax.axis_index("col")
    z, x = col // SIDE, lax.rem(col, SIDE)

    def place(r):
        return lax.rem(z + r[0], SIDE) * SIDE + lax.rem(x + r[1], SIDE)

    def to_row(delta):
        return {"row": lax.rem(row + delta, ROWS)}

    def to_col(e, sign):
        return {"col": place((e[0] * (1 if sign > 0 else SIDE - 1), e[1] * (1 if sign > 0 else SIDE - 1)))}

    barrier = pltpu.get_barrier_semaphore()
    for delta in range(1, ROWS):
        pl.semaphore_signal(barrier, inc=1, device_id=to_row(delta), device_id_type=MESH)
    for e in LINE.values():
        for sign in (1, -1):
            pl.semaphore_signal(barrier, inc=1, device_id=to_col(e, sign), device_id_type=MESH)

    order, shift = orders[row], shifts[row]
    eye = (
        lax.broadcasted_iota(jnp.int32, (B, B), 0) == lax.broadcasted_iota(jnp.int32, (B, B), 1)
    )
    for q in range(nq):
        for d in CHUNKS[q][1]:
            there = place(d)
            blk = x_ref[0, :, pl.ds(pl.multiple_of(there * B, B), B)]
            if d == (0, 0):
                blk = blk - jnp.where(eye, shift, jnp.float32(0.0))
            live = jnp.maximum(col, there) * B < order
            blk = blk * jnp.where(live, jnp.float32(1.0), jnp.float32(0.0))
            at = offset(q, d)
            if d in HALVES:
                leads = (x if d[0] == 0 else z) < SIDE // 2
                one = jnp.where(leads, jnp.float32(1.0), jnp.float32(0.0))
                turned = blk.T
                pack[q][at : at + B // 2] = blk[: B // 2] * one + turned[B // 2 :] * (1.0 - one)
            else:
                pack[q][at : at + B] = blk

    pl.semaphore_wait(barrier, ROWS - 1 + 4)

    first = {}
    for q in range(nq):
        n = chunk_rows(q) // ROWS
        for delta in range(1, ROWS):
            j = lax.rem(row + delta, ROWS)
            copy = pltpu.make_async_remote_copy(
                src_ref=pack[q].at[pl.ds(pl.multiple_of(j * n, 8), n)],
                dst_ref=parts[q].at[row],
                send_sem=s1.at[q * ROWS + delta],
                recv_sem=r1.at[q * ROWS + delta],
                device_id=to_row(delta),
                device_id_type=MESH,
            )
            copy.start()
            first[q, delta] = copy
        parts[q][row] = pack[q][pl.ds(pl.multiple_of(row * n, 8), n)]

    second = {}
    for q in range(nq):
        n = chunk_rows(q) // ROWS
        for delta in range(1, ROWS):
            first[q, delta].wait_recv()
        mine = pl.ds(pl.multiple_of(row * n, 8), n)
        for delta in range(1, ROWS):
            k = lax.rem(row + delta, ROWS)
            chosen[q][delta] = parts[q][child[k]]
            copy = pltpu.make_async_remote_copy(
                src_ref=chosen[q].at[delta],
                dst_ref=stage[q].at[0, mine],
                send_sem=s2.at[q * ROWS + delta],
                recv_sem=r2.at[q * ROWS + delta],
                device_id=to_row(delta),
                device_id_type=MESH,
            )
            copy.start()
            second[q, delta] = copy
        stage[q][0, mine] = parts[q][child[row]]

    third = {}

    def send(q, r, half, e, sign):
        n = chunk_rows(q)
        rows = {"all": pl.ds(0, n), "top": pl.ds(0, n // 2), "low": pl.ds(n // 2, n // 2)}[half]
        lands = plus(r, e, -sign)
        slot = (q * STRIPS + flat(lands)) * 2 + (1 if half == "low" else 0)
        copy = pltpu.make_async_remote_copy(
            src_ref=stage[q].at[flat(r), rows],
            dst_ref=stage[q].at[flat(lands), rows],
            send_sem=s3.at[slot],
            recv_sem=r3.at[slot],
            device_id=to_col(e, sign),
            device_id_type=MESH,
        )
        copy.start()
        third[q, lands, half] = copy

    def wait(q, r, half):
        third[q, r, half].wait_recv()

    def axes(q):
        a = LINE[CHUNKS[q][0]]
        return a, (a[1], a[0])

    def across(q, r):
        _, b = axes(q)
        send(q, r, "all", b, 1)
        send(q, r, "all", b, -1)

    for q in range(nq):
        a, b = axes(q)
        for delta in range(1, ROWS):
            second[q, delta].wait_recv()
        send(q, (0, 0), "all", a, 1)
        send(q, (0, 0), "all", a, -1)
        across(q, (0, 0))

    ssq[...] = jnp.zeros_like(ssq)

    def put(i, j, blk):
        at_i, at_j = pl.ds(pl.multiple_of(i * B, B), B), pl.ds(pl.multiple_of(j * B, B), B)
        high, low = split(blk)
        sh[at_i, at_j] = high
        sl[at_i, at_j] = low
        if i is not j:
            high, low = split(blk.T)
            sh[at_j, at_i] = high
            sl[at_j, at_i] = low

    def square(blk, weight):
        ssq[...] += weight * jnp.sum((blk * blk).reshape(-1, 8, B), axis=0)

    def unpack(q, k):
        a, b = axes(q)

        def body(t, _):
            rz, rx = t * a[0] + k * b[0], t * a[1] + k * b[1]
            r = rz * SIDE + rx
            for d in CHUNKS[q][1]:
                if d in HALVES:
                    continue
                at = offset(q, d)
                blk = stage[q][r, at : at + B]
                if d == (0, 0):
                    square(blk, 1.0)
                    put(r, r, blk)
                else:
                    square(blk, 2.0)
                    put(r, lax.rem(rz + d[0], SIDE) * SIDE + lax.rem(rx + d[1], SIDE), blk)
            return 0

        lax.fori_loop(0, SIDE, body, 0)

    def unpack_halves(q):
        for d in HALVES:
            at = offset(q, d)

            def body(t, _):
                if d[0] == 0:
                    rz, rx = t // 2, lax.rem(t, 2)
                    leads = lax.rem(x + rx, SIDE) < SIDE // 2
                else:
                    rz, rx = t // SIDE, lax.rem(t, SIDE)
                    leads = lax.rem(z + rz, SIDE) < SIDE // 2
                r = rz * SIDE + rx
                o = lax.rem(rz + d[0], SIDE) * SIDE + lax.rem(rx + d[1], SIDE)
                lead = jnp.where(leads, r, o)
                trail = r + o - lead
                blk = jnp.concatenate(
                    [stage[q][lead, at : at + B // 2], stage[q][trail, at : at + B // 2]], axis=0
                )
                square(blk, 2.0)
                put(lead, trail, blk)
                return 0

            lax.fori_loop(0, STRIPS // 2, body, 0)

    def line(q):
        a, b = axes(q)
        wait(q, plus((0, 0), a, -1), "all")
        send(q, plus((0, 0), a, -1), "top", a, 1)
        across(q, plus((0, 0), a, -1))
        wait(q, a, "all")
        send(q, a, "low", a, -1)
        across(q, a)

    def line_end(q):
        a, b = axes(q)
        far = plus((0, 0), a, 2)
        wait(q, far, "top")
        wait(q, far, "low")
        across(q, far)

    def near(q):
        a, b = axes(q)
        for k in (0, -1, 1, 2):
            r = plus((0, 0), a, k)
            wait(q, plus(r, b, -1), "all")
            send(q, plus(r, b, -1), "top", b, 1)
            wait(q, plus(r, b, 1), "all")
            send(q, plus(r, b, 1), "low", b, -1)

    def far(q):
        a, b = axes(q)
        for k in (0, -1, 1, 2):
            r = plus(plus((0, 0), a, k), b, 2)
            wait(q, r, "top")
            wait(q, r, "low")

    for q in range(nq):
        line(q)
    for q in range(nq):
        line_end(q)
    near(0)
    near(1)
    unpack(0, 0)
    unpack(1, 0)
    near(2)
    near(3)
    unpack(2, 0)
    unpack(3, 0)
    for q in range(nq):
        unpack(q, 1)
        unpack(q, 3)
    for q in range(nq):
        far(q)
        unpack(q, 2)
        if q == 1:
            unpack_halves(q)

    order_here = orders[child[row]]
    root = jnp.sqrt(jnp.full((1, TILE), order_here, jnp.int32).astype(f32))
    total = jnp.sum(jnp.sum(ssq[...], axis=0, keepdims=True), axis=1, keepdims=True)
    scale[...] = root / (2.0 * jnp.sqrt(jnp.broadcast_to(total, (1, TILE)) + 1e-06))

    def load(v, cs):
        high, low = split(v)
        lhs[0:B, cs] = high
        lhs[B : 2 * B, cs] = low

    tiles = M // TILE

    def cols(j):
        return pl.ds(pl.multiple_of(j * TILE, TILE), TILE)

    def begin(j, _):
        cs = cols(j)
        v = (sh[0:B, cs].astype(f32) + sl[0:B, cs].astype(f32)) * scale[...]
        first_strip[:, cs] = v
        load(v, cs)
        return 0

    lax.fori_loop(0, tiles, begin, 0)

    def apply(j, _):
        cs = cols(j)
        both = jnp.dot(lhs[...], sh[:, cs], preferred_element_type=f32)
        low = jnp.dot(lhs[0:B], sl[:, cs], preferred_element_type=f32)
        cur[:, cs] = (both[0:B] + both[B : 2 * B] + low) * scale[...]
        return 0

    def reload(j, _):
        load(cur[:, cols(j)], cols(j))
        return 0

    def twice(m, _):
        lax.fori_loop(0, tiles, apply, 0)
        lax.fori_loop(0, tiles, reload, 0)
        lax.fori_loop(0, tiles, apply, 0)
        is_first = m == 0
        weight = jnp.where(
            m == 1, jnp.float32(-1.125), jnp.where(m == 2, jnp.float32(0.75), jnp.float32(-0.125))
        )

        @pl.when(is_first)
        def _():
            def step(j, _):
                cs = cols(j)
                v = 1.5 * first_strip[:, cs] - 0.5 * cur[:, cs]
                res[:, cs] = 1.5 * v
                load(v, cs)
                return 0

            lax.fori_loop(0, tiles, step, 0)

        @pl.when(jnp.logical_not(is_first))
        def _():
            def step(j, _):
                cs = cols(j)
                v = cur[:, cs]
                res[:, cs] += weight * v
                load(v, cs)
                return 0

            lax.fori_loop(0, tiles, step, 0)

        return 0

    lax.fori_loop(0, 4, twice, 0)

    for rz in range(SIDE):
        for rx in range(SIDE):
            r = flat((rz, rx))
            o_ref[0, :, pl.ds(pl.multiple_of(place((rz, rx)) * B, B), B)] = (
                res[:, r * B : (r + 1) * B] * root[:, 0:B]
            )

    for copies in (first, second, third):
        for copy in copies.values():
            copy.wait_send()


def local(parent_blocks, shifts, orders, child_order):
    nq = len(CHUNKS)
    rows = [chunk_rows(q) for q in range(nq)]
    smem = pl.BlockSpec(memory_space=pltpu.SMEM)
    vmem = pl.BlockSpec(memory_space=pltpu.VMEM)
    return pl.pallas_call(
        kernel,
        out_shape=jax.ShapeDtypeStruct(parent_blocks.shape, f32),
        in_specs=[vmem, smem, smem, smem],
        out_specs=vmem,
        scratch_shapes=[pltpu.VMEM((n, B), f32) for n in rows]
        + [pltpu.VMEM((ROWS, n // ROWS, B), f32) for n in rows]
        + [pltpu.VMEM((ROWS, n // ROWS, B), f32) for n in rows]
        + [pltpu.VMEM((STRIPS, n, B), f32) for n in rows]
        + [
            pltpu.VMEM((M, M), bf16),
            pltpu.VMEM((M, M), bf16),
            pltpu.VMEM((2 * B, M), bf16),
            pltpu.VMEM((B, M), f32),
            pltpu.VMEM((B, M), f32),
            pltpu.VMEM((B, M), f32),
            pltpu.VMEM((8, B), f32),
            pltpu.VMEM((1, TILE), f32),
            pltpu.SemaphoreType.DMA((nq * ROWS,)),
            pltpu.SemaphoreType.DMA((nq * ROWS,)),
            pltpu.SemaphoreType.DMA((nq * ROWS,)),
            pltpu.SemaphoreType.DMA((nq * ROWS,)),
            pltpu.SemaphoreType.DMA((nq * STRIPS * 2,)),
            pltpu.SemaphoreType.DMA((nq * STRIPS * 2,)),
        ],
        compiler_params=pltpu.CompilerParams(
            collective_id=0, has_side_effects=True, vmem_limit_bytes=48 * 2**20
        ),
        cost_estimate=pl.CostEstimate(
            flops=8 * 3 * 2 * B * M * M, bytes_accessed=2 * 4 * B * M, transcendentals=0
        ),
        name="sign_steps",
    )(parent_blocks, shifts, orders, child_order)


def solution(mesh):
    in_specs = (P("row", "col", None), P(), P(), P())
    out_specs = P("row", "col", None)
    return jax.shard_map(local, mesh=mesh, in_specs=in_specs, out_specs=out_specs, check_vma=False)
```

```python
import jax
import jax.numpy as jnp
from jax import lax
from jax.experimental import pallas as pl
from jax.experimental.pallas import tpu as pltpu
from jax.sharding import PartitionSpec as P

MESH = pl.DeviceIdType.MESH
f32, bf16 = jnp.float32, jnp.bfloat16

SIDE = 4
STRIPS = SIDE * SIDE
ROWS = 8
B = 128
M = STRIPS * B

HALVES = ((0, 2), (2, 0), (2, 2))
CHUNKS = (
    ("x", ((0, 0), (0, 1))),
    ("z", ((2, 1),) + HALVES),
    ("x", ((1, 0), (1, 1))),
    ("z", ((1, 2), (1, 3))),
)
LINE = {"x": (0, 1), "z": (1, 0)}


def block_rows(d):
    return B // 2 if d in HALVES else B


def chunk_rows(q):
    return sum(block_rows(d) for d in CHUNKS[q][1])


def offset(q, d):
    total = 0
    for e in CHUNKS[q][1]:
        if e == d:
            return total
        total += block_rows(e)


def plus(r, e, k=1):
    return ((r[0] + k * e[0]) % SIDE, (r[1] + k * e[1]) % SIDE)


def flat(r):
    return SIDE * r[0] + r[1]


def split(v):
    high = v.astype(bf16)
    return high, (v - high.astype(f32)).astype(bf16)


def kernel(x_hbm, shifts_hbm, orders_hbm, child_hbm, o_ref, *scratch):
    nq = len(CHUNKS)
    pack, parts, chosen, stage = (scratch[i * nq : (i + 1) * nq] for i in range(4))
    sh, sl, lhs, first_strip, res, ssq, scale, s1, r1, s2, r2, s3, r3 = scratch[4 * nq : 4 * nq + 13]
    x_ref, shifts, orders, child, arg_sems = scratch[4 * nq + 13 :]

    fetches = [
        pltpu.make_async_copy(src, dst, arg_sems.at[i])
        for i, (src, dst) in enumerate(
            ((x_hbm, x_ref), (shifts_hbm, shifts), (orders_hbm, orders), (child_hbm, child))
        )
    ]
    for fetch in fetches:
        fetch.start()

    row, col = lax.axis_index("row"), lax.axis_index("col")
    z, x = col // SIDE, lax.rem(col, SIDE)

    def place(r):
        return lax.rem(z + r[0], SIDE) * SIDE + lax.rem(x + r[1], SIDE)

    def to_row(delta):
        return {"row": lax.rem(row + delta, ROWS)}

    def to_col(e, sign):
        return {"col": place((e[0] * (1 if sign > 0 else SIDE - 1), e[1] * (1 if sign > 0 else SIDE - 1)))}

    barrier = pltpu.get_barrier_semaphore()
    for delta in range(1, ROWS):
        pl.semaphore_signal(barrier, inc=1, device_id=to_row(delta), device_id_type=MESH)
    for e in LINE.values():
        for sign in (1, -1):
            pl.semaphore_signal(barrier, inc=1, device_id=to_col(e, sign), device_id_type=MESH)

    for fetch in fetches:
        fetch.wait()

    order, shift = orders[row], shifts[row]
    eye = (
        lax.broadcasted_iota(jnp.int32, (B, B), 0) == lax.broadcasted_iota(jnp.int32, (B, B), 1)
    )

    def fill(q):
        for d in CHUNKS[q][1]:
            there = place(d)
            blk = x_ref[0, :, pl.ds(pl.multiple_of(there * B, B), B)]
            if d == (0, 0):
                blk = blk - jnp.where(eye, shift, jnp.float32(0.0))
            live = jnp.maximum(col, there) * B < order
            blk = blk * jnp.where(live, jnp.float32(1.0), jnp.float32(0.0))
            at = offset(q, d)
            if d in HALVES:
                leads = (x if d[0] == 0 else z) < SIDE // 2
                one = jnp.where(leads, jnp.float32(1.0), jnp.float32(0.0))
                turned = blk.T
                pack[q][at : at + B // 2] = blk[: B // 2] * one + turned[B // 2 :] * (1.0 - one)
            else:
                pack[q][at : at + B] = blk

    first, second = {}, {}

    def spread(q):
        n = chunk_rows(q) // ROWS
        for delta in range(1, ROWS):
            j = lax.rem(row + delta, ROWS)
            copy = pltpu.make_async_remote_copy(
                src_ref=pack[q].at[pl.ds(pl.multiple_of(j * n, 8), n)],
                dst_ref=parts[q].at[row],
                send_sem=s1.at[q * ROWS + delta],
                recv_sem=r1.at[q * ROWS + delta],
                device_id=to_row(delta),
                device_id_type=MESH,
            )
            copy.start()
            first[q, delta] = copy
        parts[q][row] = pack[q][pl.ds(pl.multiple_of(row * n, 8), n)]

    def choose(q):
        n = chunk_rows(q) // ROWS
        for delta in range(1, ROWS):
            first[q, delta].wait_recv()
        mine = pl.ds(pl.multiple_of(row * n, 8), n)
        for delta in range(1, ROWS):
            k = lax.rem(row + delta, ROWS)
            chosen[q][delta] = parts[q][child[k]]
            copy = pltpu.make_async_remote_copy(
                src_ref=chosen[q].at[delta],
                dst_ref=stage[q].at[0, mine],
                send_sem=s2.at[q * ROWS + delta],
                recv_sem=r2.at[q * ROWS + delta],
                device_id=to_row(delta),
                device_id_type=MESH,
            )
            copy.start()
            second[q, delta] = copy
        stage[q][0, mine] = parts[q][child[row]]

    third = {}

    def send(q, r, half, e, sign):
        n = chunk_rows(q)
        rows = {"all": pl.ds(0, n), "top": pl.ds(0, n // 2), "low": pl.ds(n // 2, n // 2)}[half]
        lands = plus(r, e, -sign)
        slot = (q * STRIPS + flat(lands)) * 2 + (1 if half == "low" else 0)
        copy = pltpu.make_async_remote_copy(
            src_ref=stage[q].at[flat(r), rows],
            dst_ref=stage[q].at[flat(lands), rows],
            send_sem=s3.at[slot],
            recv_sem=r3.at[slot],
            device_id=to_col(e, sign),
            device_id_type=MESH,
        )
        copy.start()
        third[q, lands, half] = copy

    def wait(q, r, half):
        third[q, r, half].wait_recv()

    def axes(q):
        a = LINE[CHUNKS[q][0]]
        return a, (a[1], a[0])

    def across(q, r):
        _, b = axes(q)
        send(q, r, "all", b, 1)
        send(q, r, "all", b, -1)

    def begin_gather(q):
        a, b = axes(q)
        for delta in range(1, ROWS):
            second[q, delta].wait_recv()
        send(q, (0, 0), "all", a, 1)
        send(q, (0, 0), "all", a, -1)
        across(q, (0, 0))

    ssq[...] = jnp.zeros_like(ssq)

    def put(i, j, blk):
        at_i, at_j = pl.ds(pl.multiple_of(i * B, B), B), pl.ds(pl.multiple_of(j * B, B), B)
        high, low = split(blk)
        sh[at_i, at_j] = high
        sl[at_i, at_j] = low
        if i is not j:
            high, low = split(blk.T)
            sh[at_j, at_i] = high
            sl[at_j, at_i] = low

    def square(blk, weight):
        ssq[...] += weight * jnp.sum((blk * blk).reshape(-1, 8, B), axis=0)

    def unpack(q, k):
        a, b = axes(q)

        def body(t, _):
            rz, rx = t * a[0] + k * b[0], t * a[1] + k * b[1]
            r = rz * SIDE + rx
            for d in CHUNKS[q][1]:
                if d in HALVES:
                    continue
                at = offset(q, d)
                blk = stage[q][r, at : at + B]
                if d == (0, 0):
                    square(blk, 1.0)
                    put(r, r, blk)
                else:
                    square(blk, 2.0)
                    put(r, lax.rem(rz + d[0], SIDE) * SIDE + lax.rem(rx + d[1], SIDE), blk)
            return 0

        lax.fori_loop(0, SIDE, body, 0)

    def unpack_halves(q):
        for d in HALVES:
            at = offset(q, d)

            def body(t, _):
                if d[0] == 0:
                    rz, rx = t // 2, lax.rem(t, 2)
                    leads = lax.rem(x + rx, SIDE) < SIDE // 2
                else:
                    rz, rx = t // SIDE, lax.rem(t, SIDE)
                    leads = lax.rem(z + rz, SIDE) < SIDE // 2
                r = rz * SIDE + rx
                o = lax.rem(rz + d[0], SIDE) * SIDE + lax.rem(rx + d[1], SIDE)
                lead = jnp.where(leads, r, o)
                trail = r + o - lead
                blk = jnp.concatenate(
                    [stage[q][lead, at : at + B // 2], stage[q][trail, at : at + B // 2]], axis=0
                )
                square(blk, 2.0)
                put(lead, trail, blk)
                return 0

            lax.fori_loop(0, STRIPS // 2, body, 0)

    def line(q):
        a, b = axes(q)
        wait(q, plus((0, 0), a, -1), "all")
        send(q, plus((0, 0), a, -1), "top", a, 1)
        across(q, plus((0, 0), a, -1))
        wait(q, a, "all")
        send(q, a, "low", a, -1)
        across(q, a)

    def line_end(q):
        a, b = axes(q)
        far = plus((0, 0), a, 2)
        wait(q, far, "top")
        wait(q, far, "low")
        across(q, far)

    def near(q):
        a, b = axes(q)
        for k in (0, -1, 1, 2):
            r = plus((0, 0), a, k)
            wait(q, plus(r, b, -1), "all")
            send(q, plus(r, b, -1), "top", b, 1)
            wait(q, plus(r, b, 1), "all")
            send(q, plus(r, b, 1), "low", b, -1)

    def far(q):
        a, b = axes(q)
        for k in (0, -1, 1, 2):
            r = plus(plus((0, 0), a, k), b, 2)
            wait(q, r, "top")
            wait(q, r, "low")

    fill(0)
    fill(1)
    pl.semaphore_wait(barrier, ROWS - 1 + 4)
    spread(0)
    spread(1)
    fill(2)
    fill(3)
    choose(0)
    spread(2)
    choose(1)
    spread(3)
    begin_gather(0)
    begin_gather(1)
    choose(2)
    choose(3)
    begin_gather(2)
    begin_gather(3)
    for q in range(nq):
        line(q)
    for q in range(nq):
        line_end(q)
    near(0)
    near(1)
    unpack(0, 0)
    unpack(1, 0)
    near(2)
    near(3)
    unpack(2, 0)
    unpack(3, 0)
    for q in range(nq):
        unpack(q, 1)
        unpack(q, 3)
    for q in range(nq):
        far(q)
        unpack(q, 2)
        if q == 1:
            unpack_halves(q)

    order_here = orders[child[row]]
    root = jnp.sqrt(jnp.full((1, M), order_here, jnp.int32).astype(f32))
    total = jnp.sum(jnp.sum(ssq[...], axis=0, keepdims=True), axis=1, keepdims=True)
    scale[...] = root / (2.0 * jnp.sqrt(jnp.broadcast_to(total, (1, M)) + 1e-06))

    def load(k, v):
        high, low = split(v)
        lhs[k, 0:B] = high
        lhs[k, B : 2 * B] = low

    def product(k):
        both = jnp.dot(lhs[k], sh[...], preferred_element_type=f32)
        low = jnp.dot(lhs[k, 0:B], sl[...], preferred_element_type=f32)
        return (both[0:B] + both[B : 2 * B] + low) * scale[...]

    own = (sh[0:B].astype(f32) + sl[0:B].astype(f32)) * scale[...]
    first_strip[...] = own
    res[...] = jnp.zeros_like(res)
    load(0, own)

    def twice(m, _):
        begins = m == 0
        keep = jnp.where(begins, jnp.float32(1.5), jnp.float32(0.0))
        take = jnp.where(begins, jnp.float32(-0.5), jnp.float32(1.0))
        weight = jnp.where(
            begins,
            jnp.float32(1.5),
            jnp.where(
                m == 1, jnp.float32(-1.125), jnp.where(m == 2, jnp.float32(0.75), jnp.float32(-0.125))
            ),
        )
        load(1, product(0))
        v = keep * first_strip[...] + take * product(1)
        res[...] += weight * v
        load(0, v)
        return 0

    lax.fori_loop(0, 4, twice, 0)

    for rz in range(SIDE):
        for rx in range(SIDE):
            r = flat((rz, rx))
            o_ref[0, :, pl.ds(pl.multiple_of(place((rz, rx)) * B, B), B)] = (
                res[:, r * B : (r + 1) * B] * root[:, 0:B]
            )

    for copies in (first, second, third):
        for copy in copies.values():
            copy.wait_send()


def local(parent_blocks, shifts, orders, child_order):
    nq = len(CHUNKS)
    rows = [chunk_rows(q) for q in range(nq)]
    anywhere = pl.BlockSpec(memory_space=pl.ANY)
    return pl.pallas_call(
        kernel,
        out_shape=jax.ShapeDtypeStruct(parent_blocks.shape, f32),
        in_specs=[anywhere] * 4,
        out_specs=pl.BlockSpec(memory_space=pltpu.VMEM),
        scratch_shapes=[pltpu.VMEM((n, B), f32) for n in rows]
        + [pltpu.VMEM((ROWS, n // ROWS, B), f32) for n in rows]
        + [pltpu.VMEM((ROWS, n // ROWS, B), f32) for n in rows]
        + [pltpu.VMEM((STRIPS, n, B), f32) for n in rows]
        + [
            pltpu.VMEM((M, M), bf16),
            pltpu.VMEM((M, M), bf16),
            pltpu.VMEM((2, 2 * B, M), bf16),
            pltpu.VMEM((B, M), f32),
            pltpu.VMEM((B, M), f32),
            pltpu.VMEM((8, B), f32),
            pltpu.VMEM((1, M), f32),
            pltpu.SemaphoreType.DMA((nq * ROWS,)),
            pltpu.SemaphoreType.DMA((nq * ROWS,)),
            pltpu.SemaphoreType.DMA((nq * ROWS,)),
            pltpu.SemaphoreType.DMA((nq * ROWS,)),
            pltpu.SemaphoreType.DMA((nq * STRIPS * 2,)),
            pltpu.SemaphoreType.DMA((nq * STRIPS * 2,)),
            pltpu.VMEM(parent_blocks.shape, f32),
            pltpu.SMEM(shifts.shape, f32),
            pltpu.SMEM(orders.shape, jnp.int32),
            pltpu.SMEM(child_order.shape, jnp.int32),
            pltpu.SemaphoreType.DMA((4,)),
        ],
        compiler_params=pltpu.CompilerParams(
            collective_id=0, has_side_effects=True, vmem_limit_bytes=60 * 2**20
        ),
        cost_estimate=pl.CostEstimate(
            flops=8 * 3 * 2 * B * M * M, bytes_accessed=2 * 4 * B * M, transcendentals=0
        ),
        name="sign_steps",
    )(parent_blocks, shifts, orders, child_order)


def solution(mesh):
    in_specs = (P("row", "col", None), P(), P(), P())
    out_specs = P("row", "col", None)
    return jax.shard_map(local, mesh=mesh, in_specs=in_specs, out_specs=out_specs, check_vma=False)
```

```python
import jax
import jax.numpy as jnp
from jax import lax
from jax.experimental import pallas as pl
from jax.experimental.pallas import tpu as pltpu
from jax.sharding import PartitionSpec as P

MESH = pl.DeviceIdType.MESH
f32, bf16 = jnp.float32, jnp.bfloat16

SIDE = 4
STRIPS = SIDE * SIDE
ROWS = 8
B = 128
M = STRIPS * B

HALVES = ((0, 2), (2, 0), (2, 2))
CHUNKS = (
    ("x", ((0, 0), (0, 1))),
    ("z", ((2, 1),) + HALVES),
    ("x", ((1, 0), (1, 1))),
    ("z", ((1, 2), (1, 3))),
)
ORDER = (
    ("fill", 3), ("spread", 3), ("fill", 2), ("spread", 2), ("fill", 1), ("fill", 0), ("spread", 1), ("choose", 3),
    ("choose", 2), ("choose", 1), ("begin", 3), ("spread", 0), ("begin", 2), ("begin", 1), ("choose", 0),
    ("lineA", 2), ("lineB", 2), ("lineB", 3), ("lineB", 1), ("line_end", 2), ("begin", 0), ("lineA", 1), ("lineA", 3),
    ("unpack", 2, 0), ("lineA", 0), ("near", 1, -1, -1), ("line_end", 1), ("lineB", 0), ("near", 1, -1, 1),
    ("near", 1, 1, 1), ("near", 0, 0, -1), ("near", 2, 0, -1), ("near", 0, -1, -1), ("near", 1, 0, 1),
    ("near", 2, -1, 1), ("near", 2, 1, 1), ("line_end", 3), ("near", 1, 2, 1), ("near", 1, 1, -1), ("near", 2, 2, 1),
    ("line_end", 0), ("near", 1, 0, -1), ("unpack", 3, 0), ("unpack", 1, 0), ("near", 3, 0, -1), ("near", 0, 1, 1),
    ("near", 2, 1, -1), ("near", 0, -1, 1), ("near", 2, -1, -1), ("unpack", 1, 1), ("near", 3, -1, 1),
    ("near", 2, 0, 1), ("near", 2, 2, -1), ("near", 1, 2, -1), ("near", 3, -1, -1), ("unpack", 1, 3),
    ("unpack", 0, 0), ("near", 3, 1, 1), ("halves", 1), ("near", 3, 0, 1), ("near", 3, 1, -1), ("near", 0, 1, -1),
    ("near", 3, 2, -1), ("near", 0, 0, 1), ("near", 0, 2, -1), ("near", 3, 2, 1), ("unpack", 2, 3), ("near", 0, 2, 1),
    ("unpack", 0, 3), ("unpack", 2, 1), ("unpack", 3, 1), ("unpack", 0, 1), ("unpack", 3, 3), ("far", 1),
    ("unpack", 1, 2), ("far", 2), ("halves", 2), ("unpack", 2, 2), ("far", 0), ("far", 3), ("unpack", 3, 2),
    ("unpack", 0, 2),
)
LINE = {"x": (0, 1), "z": (1, 0)}


def block_rows(d):
    return B // 2 if d in HALVES else B


def chunk_rows(q):
    return sum(block_rows(d) for d in CHUNKS[q][1])


def offset(q, d):
    total = 0
    for e in CHUNKS[q][1]:
        if e == d:
            return total
        total += block_rows(e)


def plus(r, e, k=1):
    return ((r[0] + k * e[0]) % SIDE, (r[1] + k * e[1]) % SIDE)


def flat(r):
    return SIDE * r[0] + r[1]


def split(v):
    high = v.astype(bf16)
    return high, (v - high.astype(f32)).astype(bf16)


def kernel(x_hbm, shifts_hbm, orders_hbm, child_hbm, o_ref, *scratch):
    nq = len(CHUNKS)
    pack, parts, chosen, stage = (scratch[i * nq : (i + 1) * nq] for i in range(4))
    sh, sl, lhs, first_strip, res, ssq, scale, s1, r1, s2, r2, s3, r3 = scratch[4 * nq : 4 * nq + 13]
    x_ref, shifts, orders, child, arg_sems = scratch[4 * nq + 13 :]

    fetches = [
        pltpu.make_async_copy(src, dst, arg_sems.at[i])
        for i, (src, dst) in enumerate(
            ((x_hbm, x_ref), (shifts_hbm, shifts), (orders_hbm, orders), (child_hbm, child))
        )
    ]
    for fetch in fetches:
        fetch.start()

    row, col = lax.axis_index("row"), lax.axis_index("col")
    turned = lax.rem(row, 2)
    step_z, step_x = SIDE - (SIDE - 1) * turned, 1 + (SIDE - 1) * turned
    z, x = lax.rem(col // step_z, SIDE), lax.rem(col // step_x, SIDE)
    true_z, true_x = col // SIDE, lax.rem(col, SIDE)

    def place(r):
        return lax.rem(z + r[0], SIDE) * step_z + lax.rem(x + r[1], SIDE) * step_x

    def to_row(delta):
        return {"row": lax.rem(row + delta, ROWS)}

    def to_col(e, sign):
        return {"col": place((e[0] * (1 if sign > 0 else SIDE - 1), e[1] * (1 if sign > 0 else SIDE - 1)))}

    barrier = pltpu.get_barrier_semaphore()
    for delta in range(1, ROWS):
        pl.semaphore_signal(barrier, inc=1, device_id=to_row(delta), device_id_type=MESH)
    for e in LINE.values():
        for sign in (1, -1):
            pl.semaphore_signal(barrier, inc=1, device_id=to_col(e, sign), device_id_type=MESH)

    for fetch in fetches:
        fetch.wait()

    order, shift = orders[row], shifts[row]
    eye = (
        lax.broadcasted_iota(jnp.int32, (B, B), 0) == lax.broadcasted_iota(jnp.int32, (B, B), 1)
    )

    def fill(q):
        for d in CHUNKS[q][1]:
            there = lax.rem(true_z + d[0], SIDE) * SIDE + lax.rem(true_x + d[1], SIDE)
            blk = x_ref[0, :, pl.ds(pl.multiple_of(there * B, B), B)]
            if d == (0, 0):
                blk = blk - jnp.where(eye, shift, jnp.float32(0.0))
            live = jnp.maximum(col, there) * B < order
            blk = blk * jnp.where(live, jnp.float32(1.0), jnp.float32(0.0))
            at = offset(q, d)
            if d in HALVES:
                leads = (true_x if d[0] == 0 else true_z) < SIDE // 2
                one = jnp.where(leads, jnp.float32(1.0), jnp.float32(0.0))
                mirror = blk.T
                pack[q][at : at + B // 2] = blk[: B // 2] * one + mirror[B // 2 :] * (1.0 - one)
            else:
                pack[q][at : at + B] = blk

    first, second = {}, {}

    def spread(q):
        n = chunk_rows(q) // ROWS
        for delta in range(1, ROWS):
            j = lax.rem(row + delta, ROWS)
            copy = pltpu.make_async_remote_copy(
                src_ref=pack[q].at[pl.ds(pl.multiple_of(j * n, 8), n)],
                dst_ref=parts[q].at[row],
                send_sem=s1.at[q * ROWS + delta],
                recv_sem=r1.at[q * ROWS + delta],
                device_id=to_row(delta),
                device_id_type=MESH,
            )
            copy.start()
            first[q, delta] = copy
        parts[q][row] = pack[q][pl.ds(pl.multiple_of(row * n, 8), n)]

    def choose(q):
        n = chunk_rows(q) // ROWS
        for delta in range(1, ROWS):
            first[q, delta].wait_recv()
        mine = pl.ds(pl.multiple_of(row * n, 8), n)
        for delta in range(1, ROWS):
            k = lax.rem(row + delta, ROWS)
            chosen[q][delta] = parts[q][child[k]]
            copy = pltpu.make_async_remote_copy(
                src_ref=chosen[q].at[delta],
                dst_ref=stage[q].at[0, mine],
                send_sem=s2.at[q * ROWS + delta],
                recv_sem=r2.at[q * ROWS + delta],
                device_id=to_row(delta),
                device_id_type=MESH,
            )
            copy.start()
            second[q, delta] = copy
        stage[q][0, mine] = parts[q][child[row]]

    third = {}

    def send(q, r, half, e, sign):
        n = chunk_rows(q)
        rows = {"all": pl.ds(0, n), "top": pl.ds(0, n // 2), "low": pl.ds(n // 2, n // 2)}[half]
        lands = plus(r, e, -sign)
        slot = (q * STRIPS + flat(lands)) * 2 + (1 if half == "low" else 0)
        copy = pltpu.make_async_remote_copy(
            src_ref=stage[q].at[flat(r), rows],
            dst_ref=stage[q].at[flat(lands), rows],
            send_sem=s3.at[slot],
            recv_sem=r3.at[slot],
            device_id=to_col(e, sign),
            device_id_type=MESH,
        )
        copy.start()
        third[q, lands, half] = copy

    def wait(q, r, half):
        third[q, r, half].wait_recv()

    def axes(q):
        a = LINE[CHUNKS[q][0]]
        return a, (a[1], a[0])

    def across(q, r):
        _, b = axes(q)
        send(q, r, "all", b, 1)
        send(q, r, "all", b, -1)

    def begin_gather(q):
        a, b = axes(q)
        for delta in range(1, ROWS):
            second[q, delta].wait_recv()
        send(q, (0, 0), "all", a, 1)
        send(q, (0, 0), "all", a, -1)
        across(q, (0, 0))

    ssq[...] = jnp.zeros_like(ssq)

    def put(i, j, blk):
        at_i, at_j = pl.ds(pl.multiple_of(i * B, B), B), pl.ds(pl.multiple_of(j * B, B), B)
        high, low = split(blk)
        sh[at_i, at_j] = high
        sl[at_i, at_j] = low
        if i is not j:
            high, low = split(blk.T)
            sh[at_j, at_i] = high
            sl[at_j, at_i] = low

    def square(blk, weight):
        ssq[...] += weight * jnp.sum((blk * blk).reshape(-1, 8, B), axis=0)

    def unpack(q, k):
        if all(d in HALVES for d in CHUNKS[q][1]):
            return
        a, b = axes(q)

        def body(t, _):
            rz, rx = t * a[0] + k * b[0], t * a[1] + k * b[1]
            r = rz * SIDE + rx
            for d in CHUNKS[q][1]:
                if d in HALVES:
                    continue
                at = offset(q, d)
                blk = stage[q][r, at : at + B]
                if d == (0, 0):
                    square(blk, 1.0)
                    put(r, r, blk)
                else:
                    square(blk, 2.0)
                    dz, dx = d[0] + (d[1] - d[0]) * turned, d[1] + (d[0] - d[1]) * turned
                    put(r, lax.rem(rz + dz, SIDE) * SIDE + lax.rem(rx + dx, SIDE), blk)
            return 0

        lax.fori_loop(0, SIDE, body, 0)

    def unpack_halves(q, early):
        pairs = {
            (0, 2): ((4, 1, 1, 1),) if early else ((4, 1, 1, 0),),
            (2, 0): ((4, 2, 1, 0), (2, 1, 1, 3)) if early else ((2, 1, 1, 2),),
            (2, 2): ((4, 2, 2, 1),) if early else ((4, 2, 2, 0),),
        }
        for d in HALVES:
            at = offset(q, d) + (offset(q, d[::-1]) - offset(q, d)) * turned
            half = pl.ds(pl.multiple_of(at, B // 2), B // 2)
            for count, per, step, start in pairs[d]:

                def body(t, _):
                    rz, rx = t // per, lax.rem(t, per) * step + start
                    if d[0] == 0:
                        leads = lax.rem(x + rx, SIDE) < SIDE // 2
                    elif d[1] == 0:
                        leads = lax.rem(z + rz, SIDE) < SIDE // 2
                    else:
                        leads = lax.rem(z + rz + (x + rx - z - rz) * turned, SIDE) < SIDE // 2
                    r = rz * SIDE + rx
                    o = lax.rem(rz + d[0], SIDE) * SIDE + lax.rem(rx + d[1], SIDE)
                    lead = jnp.where(leads, r, o)
                    trail = r + o - lead
                    blk = jnp.concatenate(
                        [stage[q][lead, half], stage[q][trail, half]], axis=0
                    )
                    square(blk, 2.0)
                    put(lead, trail, blk)
                    return 0

                lax.fori_loop(0, count, body, 0)

    def line_a(q):
        a, b = axes(q)
        wait(q, plus((0, 0), a, -1), "all")
        send(q, plus((0, 0), a, -1), "top", a, 1)
        across(q, plus((0, 0), a, -1))

    def line_b(q):
        a, b = axes(q)
        wait(q, a, "all")
        send(q, a, "low", a, -1)
        across(q, a)

    def line_end(q):
        a, b = axes(q)
        far = plus((0, 0), a, 2)
        wait(q, far, "top")
        wait(q, far, "low")
        across(q, far)

    def near(q, k, side):
        a, b = axes(q)
        r = plus(plus((0, 0), a, k), b, side)
        wait(q, r, "all")
        send(q, r, "top" if side < 0 else "low", b, -side)

    def far(q):
        a, b = axes(q)
        for k in (0, -1, 1, 2):
            r = plus(plus((0, 0), a, k), b, 2)
            wait(q, r, "top")
            wait(q, r, "low")

    steps = {
        "fill": fill,
        "spread": spread,
        "choose": choose,
        "begin": begin_gather,
        "lineA": line_a,
        "lineB": line_b,
        "line_end": line_end,
        "near": near,
        "far": far,
        "unpack": unpack,
        "halves": lambda i: unpack_halves(1, i == 1),
    }
    entered = False
    for name, *args in ORDER:
        if name == "spread" and not entered:
            pl.semaphore_wait(barrier, ROWS - 1 + 4)
            entered = True
        steps[name](*args)

    order_here = orders[child[row]]
    root = jnp.sqrt(jnp.full((1, M), order_here, jnp.int32).astype(f32))
    total = jnp.sum(jnp.sum(ssq[...], axis=0, keepdims=True), axis=1, keepdims=True)
    scale[...] = root / (2.0 * jnp.sqrt(jnp.broadcast_to(total, (1, M)) + 1e-06))

    def load(k, v):
        high, low = split(v)
        lhs[k, 0:B] = high
        lhs[k, B : 2 * B] = low

    def product(k):
        both = jnp.dot(lhs[k], sh[...], preferred_element_type=f32)
        low = jnp.dot(lhs[k, 0:B], sl[...], preferred_element_type=f32)
        return (both[0:B] + both[B : 2 * B] + low) * scale[...]

    own = (sh[0:B].astype(f32) + sl[0:B].astype(f32)) * scale[...]
    first_strip[...] = own
    res[...] = jnp.zeros_like(res)
    load(0, own)

    def twice(m, _):
        begins = m == 0
        keep = jnp.where(begins, jnp.float32(1.5), jnp.float32(0.0))
        take = jnp.where(begins, jnp.float32(-0.5), jnp.float32(1.0))
        weight = jnp.where(
            begins,
            jnp.float32(1.5),
            jnp.where(
                m == 1, jnp.float32(-1.125), jnp.where(m == 2, jnp.float32(0.75), jnp.float32(-0.125))
            ),
        )
        load(1, product(0))
        v = keep * first_strip[...] + take * product(1)
        res[...] += weight * v
        load(0, v)
        return 0

    lax.fori_loop(0, 4, twice, 0)

    for rz in range(SIDE):
        for rx in range(SIDE):
            r = flat((rz, rx))
            o_ref[0, :, pl.ds(pl.multiple_of(place((rz, rx)) * B, B), B)] = (
                res[:, r * B : (r + 1) * B] * root[:, 0:B]
            )

    for copies in (first, second, third):
        for copy in copies.values():
            copy.wait_send()


def local(parent_blocks, shifts, orders, child_order):
    nq = len(CHUNKS)
    rows = [chunk_rows(q) for q in range(nq)]
    anywhere = pl.BlockSpec(memory_space=pl.ANY)
    return pl.pallas_call(
        kernel,
        out_shape=jax.ShapeDtypeStruct(parent_blocks.shape, f32),
        in_specs=[anywhere] * 4,
        out_specs=pl.BlockSpec(memory_space=pltpu.VMEM),
        scratch_shapes=[pltpu.VMEM((n, B), f32) for n in rows]
        + [pltpu.VMEM((ROWS, n // ROWS, B), f32) for n in rows]
        + [pltpu.VMEM((ROWS, n // ROWS, B), f32) for n in rows]
        + [pltpu.VMEM((STRIPS, n, B), f32) for n in rows]
        + [
            pltpu.VMEM((M, M), bf16),
            pltpu.VMEM((M, M), bf16),
            pltpu.VMEM((2, 2 * B, M), bf16),
            pltpu.VMEM((B, M), f32),
            pltpu.VMEM((B, M), f32),
            pltpu.VMEM((8, B), f32),
            pltpu.VMEM((1, M), f32),
            pltpu.SemaphoreType.DMA((nq * ROWS,)),
            pltpu.SemaphoreType.DMA((nq * ROWS,)),
            pltpu.SemaphoreType.DMA((nq * ROWS,)),
            pltpu.SemaphoreType.DMA((nq * ROWS,)),
            pltpu.SemaphoreType.DMA((nq * STRIPS * 2,)),
            pltpu.SemaphoreType.DMA((nq * STRIPS * 2,)),
            pltpu.VMEM(parent_blocks.shape, f32),
            pltpu.SMEM(shifts.shape, f32),
            pltpu.SMEM(orders.shape, jnp.int32),
            pltpu.SMEM(child_order.shape, jnp.int32),
            pltpu.SemaphoreType.DMA((4,)),
        ],
        compiler_params=pltpu.CompilerParams(
            collective_id=0, has_side_effects=True, vmem_limit_bytes=60 * 2**20
        ),
        cost_estimate=pl.CostEstimate(
            flops=8 * 3 * 2 * B * M * M, bytes_accessed=2 * 4 * B * M, transcendentals=0
        ),
        name="sign_steps",
    )(parent_blocks, shifts, orders, child_order)


def solution(mesh):
    in_specs = (P("row", "col", None), P(), P(), P())
    out_specs = P("row", "col", None)
    return jax.shard_map(local, mesh=mesh, in_specs=in_specs, out_specs=out_specs, check_vma=False)
```

```python
import jax
import jax.numpy as jnp
from jax import lax
from jax.experimental import pallas as pl
from jax.experimental.pallas import tpu as pltpu
from jax.sharding import PartitionSpec as P

MESH = pl.DeviceIdType.MESH
f32, bf16 = jnp.float32, jnp.bfloat16

SIDE = 4
STRIPS = SIDE * SIDE
ROWS = 8
B = 128
M = STRIPS * B
SPAN = M // SIDE

HALVES = ((0, 2), (2, 0), (2, 2))
CHUNKS = (
    ("x", ((0, 0), (0, 1))),
    ("z", ((2, 1),) + HALVES),
    ("x", ((1, 0), (1, 1))),
    ("z", ((1, 2), (1, 3))),
)
ORDER = (
    ("fill", 3), ("spread", 3), ("fill", 1), ("fill", 2), ("spread", 2), ("spread", 1), ("choose", 3), ("choose", 2),
    ("choose", 1), ("begin", 3), ("fill", 0), ("spread", 0), ("begin", 2), ("begin", 1), ("lineB", 3), ("choose", 0),
    ("lineA", 3), ("lineB", 2), ("lineB", 1), ("extra", 0), ("lineA", 2), ("take", 0), ("begin", 0), ("lineA", 1),
    ("line_end", 2), ("lineB", 0), ("lineA", 0), ("line_end", 1), ("near", 1, 0, 1), ("line_end", 3),
    ("near", 2, -1, -1), ("near", 2, 2, -1), ("near", 1, 1, -1), ("near", 2, -1, 1), ("near", 3, 1, -1),
    ("line_end", 0), ("near", 2, 2, 1), ("unpack", 2, 0), ("near", 1, 0, -1), ("near", 0, 1, 1), ("near", 2, 0, 1),
    ("near", 2, 1, -1), ("near", 1, 2, 1), ("near", 1, -1, -1), ("near", 1, -1, 1), ("near", 2, 1, 1),
    ("near", 2, 0, -1), ("near", 3, -1, 1), ("near", 3, 0, -1), ("near", 1, 2, -1), ("near", 1, 1, 1),
    ("unpack", 1, 1), ("near", 0, -1, -1), ("unpack", 1, 0), ("near", 0, 0, -1), ("near", 3, 0, 1), ("unpack", 2, 3),
    ("near", 3, 1, 1), ("unpack", 1, 3), ("near", 3, -1, -1), ("unpack", 0, 0), ("unpack", 2, 1), ("unpack", 3, 0),
    ("near", 3, 2, 1), ("near", 0, 0, 1), ("near", 0, 1, -1), ("near", 0, -1, 1), ("unpack", 3, 1), ("near", 0, 2, 1),
    ("near", 0, 2, -1), ("unpack", 0, 3), ("halves", 1), ("unpack", 0, 1), ("near", 3, 2, -1), ("far", 2),
    ("unpack", 3, 3), ("far", 1), ("unpack", 1, 2), ("halves", 2), ("unpack", 2, 2), ("far", 0), ("far", 3),
    ("unpack", 3, 2), ("unpack", 0, 2),
)
LINE = {"x": (0, 1), "z": (1, 0)}


DIAGONAL = (0, 0)
EXTRA = 8


def block_rows(d):
    return B // 2 if d in HALVES or d == DIAGONAL else B


def chunk_rows(q):
    return sum(block_rows(d) for d in CHUNKS[q][1])


def gather_rows(q):
    return chunk_rows(q) + (EXTRA if DIAGONAL in CHUNKS[q][1] else 0)


def offset(q, d):
    total = 0
    for e in CHUNKS[q][1]:
        if e == d:
            return total
        total += block_rows(e)


def plus(r, e, k=1):
    return ((r[0] + k * e[0]) % SIDE, (r[1] + k * e[1]) % SIDE)


def flat(r):
    return SIDE * r[0] + r[1]


def split(v):
    high = v.astype(bf16)
    return high, (v - high.astype(f32)).astype(bf16)


def kernel(x_hbm, shifts_hbm, orders_hbm, child_hbm, o_hbm, *scratch):
    nq = len(CHUNKS)
    pack, parts, chosen, stage = (scratch[i * nq : (i + 1) * nq] for i in range(4))
    sh, sl, lhs, first_strip, res, ssq, scale, s1, r1, s2, r2, s3, r3, s4, r4 = scratch[4 * nq : 4 * nq + 15]
    x_ref, shifts, orders, child, arg_sems, extra_out, extra_in, out_sems = scratch[4 * nq + 15 :]

    fetches = [
        pltpu.make_async_copy(src, dst, arg_sems.at[i])
        for i, (src, dst) in enumerate(
            ((x_hbm, x_ref), (shifts_hbm, shifts), (orders_hbm, orders), (child_hbm, child))
        )
    ]
    for fetch in fetches:
        fetch.start()

    row, col = lax.axis_index("row"), lax.axis_index("col")
    turned = lax.rem(row, 2)
    step_z, step_x = SIDE - (SIDE - 1) * turned, 1 + (SIDE - 1) * turned
    z, x = lax.rem(col // step_z, SIDE), lax.rem(col // step_x, SIDE)
    true_z, true_x = col // SIDE, lax.rem(col, SIDE)

    def place(r):
        return lax.rem(z + r[0], SIDE) * step_z + lax.rem(x + r[1], SIDE) * step_x

    def to_row(delta):
        return {"row": lax.rem(row + delta, ROWS)}

    def to_col(e, sign):
        return {"col": place((e[0] * (1 if sign > 0 else SIDE - 1), e[1] * (1 if sign > 0 else SIDE - 1)))}

    barrier = pltpu.get_barrier_semaphore()
    for delta in range(1, ROWS):
        pl.semaphore_signal(barrier, inc=1, device_id=to_row(delta), device_id_type=MESH)
    for e in LINE.values():
        for sign in (1, -1):
            pl.semaphore_signal(barrier, inc=1, device_id=to_col(e, sign), device_id_type=MESH)

    for fetch in fetches:
        fetch.wait()

    order, shift = orders[row], shifts[row]
    eye = (
        lax.broadcasted_iota(jnp.int32, (B, B), 0) == lax.broadcasted_iota(jnp.int32, (B, B), 1)
    )

    half_row = lax.broadcasted_iota(jnp.int32, (B // 2, B), 0)
    half_lane = lax.broadcasted_iota(jnp.int32, (B // 2, B), 1)
    upper = half_row <= half_lane
    lower_eye = half_lane == half_row + B // 2

    def fill(q):
        for d in CHUNKS[q][1]:
            there = lax.rem(true_z + d[0], SIDE) * SIDE + lax.rem(true_x + d[1], SIDE)
            blk = x_ref[0, :, pl.ds(pl.multiple_of(there * B, B), B)]
            if d == DIAGONAL:
                blk = blk - jnp.where(eye, shift, jnp.float32(0.0))
            live = jnp.maximum(col, there) * B < order
            blk = blk * jnp.where(live, jnp.float32(1.0), jnp.float32(0.0))
            at = offset(q, d)
            if d in HALVES:
                leads = (true_x if d[0] == 0 else true_z) < SIDE // 2
                one = jnp.where(leads, jnp.float32(1.0), jnp.float32(0.0))
                mirror = blk.T
                pack[q][at : at + B // 2] = blk[: B // 2] * one + mirror[B // 2 :] * (1.0 - one)
            elif d == DIAGONAL:
                top, bottom = blk[: B // 2], blk[B // 2 :]
                pack[q][at : at + B // 2] = jnp.where(upper, top, pltpu.roll(bottom, B // 2, 1))
                last = jnp.sum(jnp.where(lower_eye, bottom, 0.0), axis=0, keepdims=True)
                extra_out[...] = jnp.broadcast_to(last, (EXTRA, B))
            else:
                pack[q][at : at + B] = blk

    first, second = {}, {}

    def spread(q):
        n = chunk_rows(q) // ROWS
        for delta in range(1, ROWS):
            j = lax.rem(row + delta, ROWS)
            copy = pltpu.make_async_remote_copy(
                src_ref=pack[q].at[pl.ds(pl.multiple_of(j * n, 8), n)],
                dst_ref=parts[q].at[row],
                send_sem=s1.at[q * ROWS + delta],
                recv_sem=r1.at[q * ROWS + delta],
                device_id=to_row(delta),
                device_id_type=MESH,
            )
            copy.start()
            first[q, delta] = copy
        parts[q][row] = pack[q][pl.ds(pl.multiple_of(row * n, 8), n)]

    def choose(q):
        n = chunk_rows(q) // ROWS
        for delta in range(1, ROWS):
            first[q, delta].wait_recv()
        mine = pl.ds(pl.multiple_of(row * n, 8), n)
        for delta in range(1, ROWS):
            k = lax.rem(row + delta, ROWS)
            chosen[q][delta] = parts[q][child[k]]
            copy = pltpu.make_async_remote_copy(
                src_ref=chosen[q].at[delta],
                dst_ref=stage[q].at[0, mine],
                send_sem=s2.at[q * ROWS + delta],
                recv_sem=r2.at[q * ROWS + delta],
                device_id=to_row(delta),
                device_id_type=MESH,
            )
            copy.start()
            second[q, delta] = copy
        stage[q][0, mine] = parts[q][child[row]]

    fourth = {}

    def extra():
        for delta in range(1, ROWS):
            copy = pltpu.make_async_remote_copy(
                src_ref=extra_out,
                dst_ref=extra_in.at[row],
                send_sem=s4.at[delta],
                recv_sem=r4.at[delta],
                device_id=to_row(delta),
                device_id_type=MESH,
            )
            copy.start()
            fourth[delta] = copy
        extra_in[row] = extra_out[...]

    def take():
        for delta in range(1, ROWS):
            fourth[delta].wait_recv()
        stage[0][0, chunk_rows(0) :] = extra_in[child[row]]

    third = {}

    def send(q, r, half, e, sign):
        n = gather_rows(q)
        cut = (n // 2 + 7) // 8 * 8
        rows = {"all": pl.ds(0, n), "top": pl.ds(0, cut), "low": pl.ds(cut, n - cut)}[half]
        lands = plus(r, e, -sign)
        slot = (q * STRIPS + flat(lands)) * 2 + (1 if half == "low" else 0)
        copy = pltpu.make_async_remote_copy(
            src_ref=stage[q].at[flat(r), rows],
            dst_ref=stage[q].at[flat(lands), rows],
            send_sem=s3.at[slot],
            recv_sem=r3.at[slot],
            device_id=to_col(e, sign),
            device_id_type=MESH,
        )
        copy.start()
        third[q, lands, half] = copy

    def wait(q, r, half):
        third[q, r, half].wait_recv()

    def axes(q):
        a = LINE[CHUNKS[q][0]]
        return a, (a[1], a[0])

    def across(q, r):
        _, b = axes(q)
        send(q, r, "all", b, 1)
        send(q, r, "all", b, -1)

    def begin_gather(q):
        a, b = axes(q)
        for delta in range(1, ROWS):
            second[q, delta].wait_recv()
        send(q, (0, 0), "all", a, 1)
        send(q, (0, 0), "all", a, -1)
        across(q, (0, 0))

    ssq[...] = jnp.zeros_like(ssq)

    def put(i, j, blk):
        at_i, at_j = pl.ds(pl.multiple_of(i * B, B), B), pl.ds(pl.multiple_of(j * B, B), B)
        high, low = split(blk)
        sh[at_i, at_j] = high
        sl[at_i, at_j] = low
        if i is not j:
            high, low = split(blk.T)
            sh[at_j, at_i] = high
            sl[at_j, at_i] = low

    def square(blk, weight):
        ssq[...] += weight * jnp.sum((blk * blk).reshape(-1, 8, B), axis=0)

    def diagonal(part, last):
        mirror = jnp.concatenate([part, jnp.zeros_like(part)], axis=0).T
        above = mirror[: B // 2]
        top = jnp.where(upper, part, above)
        right = jnp.where(
            half_lane < half_row + B // 2, pltpu.roll(part, B // 2, 1), pltpu.roll(above, B // 2, 1)
        )
        right = jnp.where(lower_eye, last, right)
        bottom = jnp.where(half_lane < B // 2, mirror[B // 2 :], right)
        return jnp.concatenate([top, bottom], axis=0)

    def unpack(q, k):
        if all(d in HALVES for d in CHUNKS[q][1]):
            return
        a, b = axes(q)

        def body(t, _):
            rz, rx = t * a[0] + k * b[0], t * a[1] + k * b[1]
            r = rz * SIDE + rx
            for d in CHUNKS[q][1]:
                if d in HALVES:
                    continue
                at = offset(q, d)
                if d == DIAGONAL:
                    blk = diagonal(stage[q][r, at : at + B // 2], stage[q][r, chunk_rows(q) :][0:1])
                    square(blk, 1.0)
                    put(r, r, blk)
                else:
                    blk = stage[q][r, at : at + B]
                    square(blk, 2.0)
                    dz, dx = d[0] + (d[1] - d[0]) * turned, d[1] + (d[0] - d[1]) * turned
                    put(r, lax.rem(rz + dz, SIDE) * SIDE + lax.rem(rx + dx, SIDE), blk)
            return 0

        lax.fori_loop(0, SIDE, body, 0)

    def unpack_halves(q, early):
        pairs = {
            (0, 2): ((4, 1, 1, 1),) if early else ((4, 1, 1, 0),),
            (2, 0): ((4, 2, 1, 0), (2, 1, 1, 3)) if early else ((2, 1, 1, 2),),
            (2, 2): ((4, 2, 2, 1),) if early else ((4, 2, 2, 0),),
        }
        for d in HALVES:
            at = offset(q, d) + (offset(q, d[::-1]) - offset(q, d)) * turned
            half = pl.ds(pl.multiple_of(at, B // 2), B // 2)
            for count, per, step, start in pairs[d]:

                def body(t, _):
                    rz, rx = t // per, lax.rem(t, per) * step + start
                    if d[0] == 0:
                        leads = lax.rem(x + rx, SIDE) < SIDE // 2
                    elif d[1] == 0:
                        leads = lax.rem(z + rz, SIDE) < SIDE // 2
                    else:
                        leads = lax.rem(z + rz + (x + rx - z - rz) * turned, SIDE) < SIDE // 2
                    r = rz * SIDE + rx
                    o = lax.rem(rz + d[0], SIDE) * SIDE + lax.rem(rx + d[1], SIDE)
                    lead = jnp.where(leads, r, o)
                    trail = r + o - lead
                    blk = jnp.concatenate(
                        [stage[q][lead, half], stage[q][trail, half]], axis=0
                    )
                    square(blk, 2.0)
                    put(lead, trail, blk)
                    return 0

                lax.fori_loop(0, count, body, 0)

    def line_a(q):
        a, b = axes(q)
        wait(q, plus((0, 0), a, -1), "all")
        send(q, plus((0, 0), a, -1), "top", a, 1)
        across(q, plus((0, 0), a, -1))

    def line_b(q):
        a, b = axes(q)
        wait(q, a, "all")
        send(q, a, "low", a, -1)
        across(q, a)

    def line_end(q):
        a, b = axes(q)
        far = plus((0, 0), a, 2)
        wait(q, far, "top")
        wait(q, far, "low")
        across(q, far)

    def near(q, k, side):
        a, b = axes(q)
        r = plus(plus((0, 0), a, k), b, side)
        wait(q, r, "all")
        send(q, r, "top" if side < 0 else "low", b, -side)

    def far(q):
        a, b = axes(q)
        for k in (0, -1, 1, 2):
            r = plus(plus((0, 0), a, k), b, 2)
            wait(q, r, "top")
            wait(q, r, "low")

    steps = {
        "fill": fill,
        "spread": spread,
        "choose": choose,
        "extra": lambda _: extra(),
        "take": lambda _: take(),
        "begin": begin_gather,
        "lineA": line_a,
        "lineB": line_b,
        "line_end": line_end,
        "near": near,
        "far": far,
        "unpack": unpack,
        "halves": lambda i: unpack_halves(1, i == 1),
    }
    entered = False
    for name, *args in ORDER:
        if name == "spread" and not entered:
            pl.semaphore_wait(barrier, ROWS - 1 + 4)
            entered = True
        steps[name](*args)

    order_here = orders[child[row]]
    root = jnp.sqrt(jnp.full((1, M), order_here, jnp.int32).astype(f32))
    total = jnp.sum(jnp.sum(ssq[...], axis=0, keepdims=True), axis=1, keepdims=True)
    scale[...] = root / (2.0 * jnp.sqrt(jnp.broadcast_to(total, (1, M)) + 1e-06))

    def load(k, v, cs=slice(None)):
        high, low = split(v)
        lhs[k, 0:B, cs] = high
        lhs[k, B : 2 * B, cs] = low

    def quarter(k, cs):
        both = jnp.dot(lhs[k], sh[:, cs], preferred_element_type=f32)
        low = jnp.dot(lhs[k, 0:B], sl[:, cs], preferred_element_type=f32)
        return (both[0:B] + both[B : 2 * B] + low) * scale[:, cs]

    spans = [pl.ds(j * SPAN, SPAN) for j in range(SIDE)]

    own = (sh[0:B].astype(f32) + sl[0:B].astype(f32)) * scale[...]
    first_strip[...] = own
    res[...] = jnp.zeros_like(res)
    load(0, own)

    def twice(m, _):
        begins = m == 0
        keep = jnp.where(begins, jnp.float32(1.5), jnp.float32(0.0))
        take = jnp.where(begins, jnp.float32(-0.5), jnp.float32(1.0))
        weight = jnp.where(
            begins, jnp.float32(1.5), jnp.where(m == 1, jnp.float32(-1.125), jnp.float32(0.75))
        )
        for cs in spans:
            load(1, quarter(0, cs), cs)
        for cs in spans:
            v = keep * first_strip[:, cs] + take * quarter(1, cs)
            res[:, cs] += weight * v
            load(0, v, cs)
        return 0

    lax.fori_loop(0, 3, twice, 0)

    for cs in spans:
        load(1, quarter(0, cs), cs)
    leaving = []
    for j, cs in enumerate(spans):
        res[:, cs] = (res[:, cs] - 0.125 * quarter(1, cs)) * root[:, 0:SPAN]
        for rx in range(SIDE):
            r = flat((j, rx))
            copy = pltpu.make_async_copy(
                res.at[:, pl.ds(r * B, B)],
                o_hbm.at[0, :, pl.ds(pl.multiple_of(place((j, rx)) * B, B), B)],
                out_sems.at[r],
            )
            copy.start()
            leaving.append(copy)
    for copy in leaving:
        copy.wait()

    for copies in (first, second, third, fourth):
        for copy in copies.values():
            copy.wait_send()


def local(parent_blocks, shifts, orders, child_order):
    nq = len(CHUNKS)
    rows = [chunk_rows(q) for q in range(nq)]
    anywhere = pl.BlockSpec(memory_space=pl.ANY)
    return pl.pallas_call(
        kernel,
        out_shape=jax.ShapeDtypeStruct(parent_blocks.shape, f32),
        in_specs=[anywhere] * 4,
        out_specs=anywhere,
        scratch_shapes=[pltpu.VMEM((n, B), f32) for n in rows]
        + [pltpu.VMEM((ROWS, n // ROWS, B), f32) for n in rows]
        + [pltpu.VMEM((ROWS, n // ROWS, B), f32) for n in rows]
        + [pltpu.VMEM((STRIPS, gather_rows(q), B), f32) for q in range(nq)]
        + [
            pltpu.VMEM((M, M), bf16),
            pltpu.VMEM((M, M), bf16),
            pltpu.VMEM((2, 2 * B, M), bf16),
            pltpu.VMEM((B, M), f32),
            pltpu.VMEM((B, M), f32),
            pltpu.VMEM((8, B), f32),
            pltpu.VMEM((1, M), f32),
            pltpu.SemaphoreType.DMA((nq * ROWS,)),
            pltpu.SemaphoreType.DMA((nq * ROWS,)),
            pltpu.SemaphoreType.DMA((nq * ROWS,)),
            pltpu.SemaphoreType.DMA((nq * ROWS,)),
            pltpu.SemaphoreType.DMA((nq * STRIPS * 2,)),
            pltpu.SemaphoreType.DMA((nq * STRIPS * 2,)),
            pltpu.SemaphoreType.DMA((ROWS,)),
            pltpu.SemaphoreType.DMA((ROWS,)),
            pltpu.VMEM(parent_blocks.shape, f32),
            pltpu.SMEM(shifts.shape, f32),
            pltpu.SMEM(orders.shape, jnp.int32),
            pltpu.SMEM(child_order.shape, jnp.int32),
            pltpu.SemaphoreType.DMA((4,)),
            pltpu.VMEM((EXTRA, B), f32),
            pltpu.VMEM((ROWS, EXTRA, B), f32),
            pltpu.SemaphoreType.DMA((STRIPS,)),
        ],
        compiler_params=pltpu.CompilerParams(
            collective_id=0, has_side_effects=True, vmem_limit_bytes=60 * 2**20
        ),
        cost_estimate=pl.CostEstimate(
            flops=8 * 3 * 2 * B * M * M, bytes_accessed=2 * 4 * B * M, transcendentals=0
        ),
        name="sign_steps",
    )(parent_blocks, shifts, orders, child_order)


def solution(mesh):
    in_specs = (P("row", "col", None), P(), P(), P())
    out_specs = P("row", "col", None)
    return jax.shard_map(local, mesh=mesh, in_specs=in_specs, out_specs=out_specs, check_vma=False)
```

```python
import jax
import jax.numpy as jnp
from jax import lax
from jax.experimental import pallas as pl
from jax.experimental.pallas import tpu as pltpu
from jax.sharding import PartitionSpec as P

MESH = pl.DeviceIdType.MESH
f32, bf16 = jnp.float32, jnp.bfloat16

SIDE = 4
STRIPS = SIDE * SIDE
ROWS = 8
B = 128
M = STRIPS * B
SPAN = M // SIDE

HALVES = ((0, 2), (2, 0), (2, 2))
CHUNKS = (
    ("x", ((0, 0), (0, 1))),
    ("z", ((2, 1),) + HALVES),
    ("x", ((1, 0), (1, 1))),
    ("z", ((1, 2), (1, 3))),
)
ORDER = (
    ("fill", 3), ("spread", 3), ("fill", 1), ("fill", 2), ("spread", 2), ("spread", 1), ("choose", 3), ("choose", 2),
    ("choose", 1), ("begin", 3), ("fill", 0), ("spread", 0), ("begin", 2), ("begin", 1), ("lineB", 3), ("choose", 0),
    ("lineA", 3), ("lineB", 2), ("lineB", 1), ("extra", 0), ("lineA", 2), ("take", 0), ("begin", 0), ("lineA", 1),
    ("line_end", 2), ("lineB", 0), ("lineA", 0), ("line_end", 1), ("near", 1, 0, 1), ("line_end", 3),
    ("near", 2, -1, -1), ("near", 2, 2, -1), ("near", 1, 1, -1), ("near", 2, -1, 1), ("near", 3, 1, -1),
    ("line_end", 0), ("near", 2, 2, 1), ("unpack", 2, 0), ("near", 1, 0, -1), ("near", 0, 1, 1), ("near", 2, 0, 1),
    ("near", 2, 1, -1), ("near", 1, 2, 1), ("near", 1, -1, -1), ("near", 1, -1, 1), ("near", 2, 1, 1),
    ("near", 2, 0, -1), ("near", 3, -1, 1), ("near", 3, 0, -1), ("near", 1, 2, -1), ("near", 1, 1, 1),
    ("unpack", 1, 1), ("near", 0, -1, -1), ("unpack", 1, 0), ("near", 0, 0, -1), ("near", 3, 0, 1), ("unpack", 2, 3),
    ("near", 3, 1, 1), ("unpack", 1, 3), ("near", 3, -1, -1), ("unpack", 0, 0), ("unpack", 2, 1), ("unpack", 3, 0),
    ("near", 3, 2, 1), ("near", 0, 0, 1), ("near", 0, 1, -1), ("near", 0, -1, 1), ("unpack", 3, 1), ("near", 0, 2, 1),
    ("near", 0, 2, -1), ("unpack", 0, 3), ("halves", 1), ("unpack", 0, 1), ("near", 3, 2, -1), ("far", 2),
    ("unpack", 3, 3), ("far", 1), ("unpack", 1, 2), ("halves", 2), ("unpack", 2, 2), ("far", 0), ("far", 3),
    ("unpack", 3, 2), ("unpack", 0, 2),
)
LINE = {"x": (0, 1), "z": (1, 0)}


DIAGONAL = (0, 0)
EXTRA = 8


def block_rows(d):
    return B // 2 if d in HALVES or d == DIAGONAL else B


def chunk_rows(q):
    return sum(block_rows(d) for d in CHUNKS[q][1])


def gather_rows(q):
    return chunk_rows(q) + (EXTRA if DIAGONAL in CHUNKS[q][1] else 0)


def offset(q, d):
    total = 0
    for e in CHUNKS[q][1]:
        if e == d:
            return total
        total += block_rows(e)


def plus(r, e, k=1):
    return ((r[0] + k * e[0]) % SIDE, (r[1] + k * e[1]) % SIDE)


def flat(r):
    return SIDE * r[0] + r[1]


def split(v):
    high = v.astype(bf16)
    return high, (v - high.astype(f32)).astype(bf16)


def kernel(x_hbm, shifts_hbm, orders_hbm, child_hbm, o_hbm, *scratch):
    nq = len(CHUNKS)
    pack, parts, chosen, stage = (scratch[i * nq : (i + 1) * nq] for i in range(4))
    sh, sl, lhs, strip, ssq, scale, s1, r1, s2, r2, s3, r3, s4, r4 = scratch[4 * nq : 4 * nq + 14]
    x_ref, shifts, orders, child, arg_sems, extra_out, extra_in, out_sems = scratch[4 * nq + 14 :]

    fetches = [
        pltpu.make_async_copy(src, dst, arg_sems.at[i])
        for i, (src, dst) in enumerate(
            ((x_hbm, x_ref), (shifts_hbm, shifts), (orders_hbm, orders), (child_hbm, child))
        )
    ]
    for fetch in fetches:
        fetch.start()

    row, col = lax.axis_index("row"), lax.axis_index("col")
    turned = lax.rem(row, 2)
    step_z, step_x = SIDE - (SIDE - 1) * turned, 1 + (SIDE - 1) * turned
    z, x = lax.rem(col // step_z, SIDE), lax.rem(col // step_x, SIDE)
    true_z, true_x = col // SIDE, lax.rem(col, SIDE)

    def place(r):
        return lax.rem(z + r[0], SIDE) * step_z + lax.rem(x + r[1], SIDE) * step_x

    def to_row(delta):
        return {"row": lax.rem(row + delta, ROWS)}

    def to_col(e, sign):
        return {"col": place((e[0] * (1 if sign > 0 else SIDE - 1), e[1] * (1 if sign > 0 else SIDE - 1)))}

    barrier = pltpu.get_barrier_semaphore()
    for delta in range(1, ROWS):
        pl.semaphore_signal(barrier, inc=1, device_id=to_row(delta), device_id_type=MESH)
    for e in LINE.values():
        for sign in (1, -1):
            pl.semaphore_signal(barrier, inc=1, device_id=to_col(e, sign), device_id_type=MESH)

    for fetch in fetches:
        fetch.wait()

    order, shift = orders[row], shifts[row]
    eye = (
        lax.broadcasted_iota(jnp.int32, (B, B), 0) == lax.broadcasted_iota(jnp.int32, (B, B), 1)
    )

    half_row = lax.broadcasted_iota(jnp.int32, (B // 2, B), 0)
    half_lane = lax.broadcasted_iota(jnp.int32, (B // 2, B), 1)
    upper = half_row <= half_lane
    lower_eye = half_lane == half_row + B // 2

    def fill(q):
        for d in CHUNKS[q][1]:
            there = lax.rem(true_z + d[0], SIDE) * SIDE + lax.rem(true_x + d[1], SIDE)
            blk = x_ref[0, :, pl.ds(pl.multiple_of(there * B, B), B)]
            if d == DIAGONAL:
                blk = blk - jnp.where(eye, shift, jnp.float32(0.0))
            live = jnp.maximum(col, there) * B < order
            blk = blk * jnp.where(live, jnp.float32(1.0), jnp.float32(0.0))
            at = offset(q, d)
            if d in HALVES:
                leads = (true_x if d[0] == 0 else true_z) < SIDE // 2
                one = jnp.where(leads, jnp.float32(1.0), jnp.float32(0.0))
                mirror = blk.T
                pack[q][at : at + B // 2] = blk[: B // 2] * one + mirror[B // 2 :] * (1.0 - one)
            elif d == DIAGONAL:
                top, bottom = blk[: B // 2], blk[B // 2 :]
                pack[q][at : at + B // 2] = jnp.where(upper, top, pltpu.roll(bottom, B // 2, 1))
                last = jnp.sum(jnp.where(lower_eye, bottom, 0.0), axis=0, keepdims=True)
                extra_out[...] = jnp.broadcast_to(last, (EXTRA, B))
            else:
                pack[q][at : at + B] = blk

    first, second = {}, {}

    def spread(q):
        n = chunk_rows(q) // ROWS
        for delta in range(1, ROWS):
            j = lax.rem(row + delta, ROWS)
            copy = pltpu.make_async_remote_copy(
                src_ref=pack[q].at[pl.ds(pl.multiple_of(j * n, 8), n)],
                dst_ref=parts[q].at[row],
                send_sem=s1.at[q * ROWS + delta],
                recv_sem=r1.at[q * ROWS + delta],
                device_id=to_row(delta),
                device_id_type=MESH,
            )
            copy.start()
            first[q, delta] = copy
        parts[q][row] = pack[q][pl.ds(pl.multiple_of(row * n, 8), n)]

    def choose(q):
        n = chunk_rows(q) // ROWS
        for delta in range(1, ROWS):
            first[q, delta].wait_recv()
        mine = pl.ds(pl.multiple_of(row * n, 8), n)
        for delta in range(1, ROWS):
            k = lax.rem(row + delta, ROWS)
            chosen[q][delta] = parts[q][child[k]]
            copy = pltpu.make_async_remote_copy(
                src_ref=chosen[q].at[delta],
                dst_ref=stage[q].at[0, mine],
                send_sem=s2.at[q * ROWS + delta],
                recv_sem=r2.at[q * ROWS + delta],
                device_id=to_row(delta),
                device_id_type=MESH,
            )
            copy.start()
            second[q, delta] = copy
        stage[q][0, mine] = parts[q][child[row]]

    fourth = {}

    def extra():
        for delta in range(1, ROWS):
            copy = pltpu.make_async_remote_copy(
                src_ref=extra_out,
                dst_ref=extra_in.at[row],
                send_sem=s4.at[delta],
                recv_sem=r4.at[delta],
                device_id=to_row(delta),
                device_id_type=MESH,
            )
            copy.start()
            fourth[delta] = copy
        extra_in[row] = extra_out[...]

    def take():
        for delta in range(1, ROWS):
            fourth[delta].wait_recv()
        stage[0][0, chunk_rows(0) :] = extra_in[child[row]]

    third = {}

    def send(q, r, half, e, sign):
        n = gather_rows(q)
        cut = (n // 2 + 7) // 8 * 8
        rows = {"all": pl.ds(0, n), "top": pl.ds(0, cut), "low": pl.ds(cut, n - cut)}[half]
        lands = plus(r, e, -sign)
        slot = (q * STRIPS + flat(lands)) * 2 + (1 if half == "low" else 0)
        copy = pltpu.make_async_remote_copy(
            src_ref=stage[q].at[flat(r), rows],
            dst_ref=stage[q].at[flat(lands), rows],
            send_sem=s3.at[slot],
            recv_sem=r3.at[slot],
            device_id=to_col(e, sign),
            device_id_type=MESH,
        )
        copy.start()
        third[q, lands, half] = copy

    def wait(q, r, half):
        third[q, r, half].wait_recv()

    def axes(q):
        a = LINE[CHUNKS[q][0]]
        return a, (a[1], a[0])

    def across(q, r):
        _, b = axes(q)
        send(q, r, "all", b, 1)
        send(q, r, "all", b, -1)

    def begin_gather(q):
        a, b = axes(q)
        for delta in range(1, ROWS):
            second[q, delta].wait_recv()
        send(q, (0, 0), "all", a, 1)
        send(q, (0, 0), "all", a, -1)
        across(q, (0, 0))

    ssq[...] = jnp.zeros_like(ssq)

    def put(i, j, blk):
        at_i, at_j = pl.ds(pl.multiple_of(i * B, B), B), pl.ds(pl.multiple_of(j * B, B), B)
        high, low = split(blk)
        sh[at_i, at_j] = high
        sl[at_i, at_j] = low
        if i is not j:
            high, low = split(blk.T)
            sh[at_j, at_i] = high
            sl[at_j, at_i] = low

    def square(blk, weight):
        ssq[...] += weight * jnp.sum((blk * blk).reshape(-1, 8, B), axis=0)

    def diagonal(part, last):
        mirror = jnp.concatenate([part, jnp.zeros_like(part)], axis=0).T
        above = mirror[: B // 2]
        top = jnp.where(upper, part, above)
        right = jnp.where(
            half_lane < half_row + B // 2, pltpu.roll(part, B // 2, 1), pltpu.roll(above, B // 2, 1)
        )
        right = jnp.where(lower_eye, last, right)
        bottom = jnp.where(half_lane < B // 2, mirror[B // 2 :], right)
        return jnp.concatenate([top, bottom], axis=0)

    def unpack(q, k):
        if all(d in HALVES for d in CHUNKS[q][1]):
            return
        a, b = axes(q)

        def body(t, _):
            rz, rx = t * a[0] + k * b[0], t * a[1] + k * b[1]
            r = rz * SIDE + rx
            for d in CHUNKS[q][1]:
                if d in HALVES:
                    continue
                at = offset(q, d)
                if d == DIAGONAL:
                    blk = diagonal(stage[q][r, at : at + B // 2], stage[q][r, chunk_rows(q) :][0:1])
                    square(blk, 1.0)
                    put(r, r, blk)
                else:
                    blk = stage[q][r, at : at + B]
                    square(blk, 2.0)
                    dz, dx = d[0] + (d[1] - d[0]) * turned, d[1] + (d[0] - d[1]) * turned
                    put(r, lax.rem(rz + dz, SIDE) * SIDE + lax.rem(rx + dx, SIDE), blk)
            return 0

        lax.fori_loop(0, SIDE, body, 0)

    def unpack_halves(q, early):
        pairs = {
            (0, 2): ((4, 1, 1, 1),) if early else ((4, 1, 1, 0),),
            (2, 0): ((4, 2, 1, 0), (2, 1, 1, 3)) if early else ((2, 1, 1, 2),),
            (2, 2): ((4, 2, 2, 1),) if early else ((4, 2, 2, 0),),
        }
        for d in HALVES:
            at = offset(q, d) + (offset(q, d[::-1]) - offset(q, d)) * turned
            half = pl.ds(pl.multiple_of(at, B // 2), B // 2)
            for count, per, step, start in pairs[d]:

                def body(t, _):
                    rz, rx = t // per, lax.rem(t, per) * step + start
                    if d[0] == 0:
                        leads = lax.rem(x + rx, SIDE) < SIDE // 2
                    elif d[1] == 0:
                        leads = lax.rem(z + rz, SIDE) < SIDE // 2
                    else:
                        leads = lax.rem(z + rz + (x + rx - z - rz) * turned, SIDE) < SIDE // 2
                    r = rz * SIDE + rx
                    o = lax.rem(rz + d[0], SIDE) * SIDE + lax.rem(rx + d[1], SIDE)
                    lead = jnp.where(leads, r, o)
                    trail = r + o - lead
                    blk = jnp.concatenate(
                        [stage[q][lead, half], stage[q][trail, half]], axis=0
                    )
                    square(blk, 2.0)
                    put(lead, trail, blk)
                    return 0

                lax.fori_loop(0, count, body, 0)

    def line_a(q):
        a, b = axes(q)
        wait(q, plus((0, 0), a, -1), "all")
        send(q, plus((0, 0), a, -1), "top", a, 1)
        across(q, plus((0, 0), a, -1))

    def line_b(q):
        a, b = axes(q)
        wait(q, a, "all")
        send(q, a, "low", a, -1)
        across(q, a)

    def line_end(q):
        a, b = axes(q)
        far = plus((0, 0), a, 2)
        wait(q, far, "top")
        wait(q, far, "low")
        across(q, far)

    def near(q, k, side):
        a, b = axes(q)
        r = plus(plus((0, 0), a, k), b, side)
        wait(q, r, "all")
        send(q, r, "top" if side < 0 else "low", b, -side)

    def far(q):
        a, b = axes(q)
        for k in (0, -1, 1, 2):
            r = plus(plus((0, 0), a, k), b, 2)
            wait(q, r, "top")
            wait(q, r, "low")

    steps = {
        "fill": fill,
        "spread": spread,
        "choose": choose,
        "extra": lambda _: extra(),
        "take": lambda _: take(),
        "begin": begin_gather,
        "lineA": line_a,
        "lineB": line_b,
        "line_end": line_end,
        "near": near,
        "far": far,
        "unpack": unpack,
        "halves": lambda i: unpack_halves(1, i == 1),
    }
    entered = False
    for name, *args in ORDER:
        if name == "spread" and not entered:
            pl.semaphore_wait(barrier, ROWS - 1 + 4)
            entered = True
        steps[name](*args)

    order_here = orders[child[row]]
    root = jnp.sqrt(jnp.full((1, M), order_here, jnp.int32).astype(f32))
    total = jnp.sum(jnp.sum(ssq[...], axis=0, keepdims=True), axis=1, keepdims=True)
    scale[...] = root / (2.0 * jnp.sqrt(jnp.broadcast_to(total, (1, M)) + 1e-06))

    def load(k, v, cs=slice(None)):
        high, low = split(v)
        lhs[k, 0:B, cs] = high
        lhs[k, B : 2 * B, cs] = low

    def quarter(k, cs):
        both = jnp.dot(lhs[k], sh[:, cs], preferred_element_type=f32)
        low = jnp.dot(lhs[k, 0:B], sl[:, cs], preferred_element_type=f32)
        return (both[0:B] + both[B : 2 * B] + low) * scale[:, cs]

    spans = [pl.ds(j * SPAN, SPAN) for j in range(SIDE)]

    for cs in spans:
        own = (sh[0:B, cs].astype(f32) + sl[0:B, cs].astype(f32)) * scale[:, cs]
        strip[:, cs] = own
        load(0, own, cs)

    for cs in spans:
        load(1, quarter(0, cs), cs)
    for cs in spans:
        v = 1.5 * strip[:, cs] - 0.5 * quarter(1, cs)
        strip[:, cs] = v
        load(0, -0.125 * v, cs)

    def horner(m, _):
        weight = jnp.where(m == 0, jnp.float32(0.75), jnp.float32(-1.125))
        for cs in spans:
            load(1, quarter(0, cs), cs)
        for cs in spans:
            load(0, quarter(1, cs) + weight * strip[:, cs], cs)
        return 0

    lax.fori_loop(0, 2, horner, 0)

    for cs in spans:
        load(1, quarter(0, cs), cs)
    leaving = []
    for j, cs in enumerate(spans):
        strip[:, cs] = (quarter(1, cs) + 1.5 * strip[:, cs]) * root[:, 0:SPAN]
        for rx in range(SIDE):
            r = flat((j, rx))
            copy = pltpu.make_async_copy(
                strip.at[:, pl.ds(r * B, B)],
                o_hbm.at[0, :, pl.ds(pl.multiple_of(place((j, rx)) * B, B), B)],
                out_sems.at[r],
            )
            copy.start()
            leaving.append(copy)
    for copy in leaving:
        copy.wait()

    for copies in (first, second, third, fourth):
        for copy in copies.values():
            copy.wait_send()


def local(parent_blocks, shifts, orders, child_order):
    nq = len(CHUNKS)
    rows = [chunk_rows(q) for q in range(nq)]
    anywhere = pl.BlockSpec(memory_space=pl.ANY)
    return pl.pallas_call(
        kernel,
        out_shape=jax.ShapeDtypeStruct(parent_blocks.shape, f32),
        in_specs=[anywhere] * 4,
        out_specs=anywhere,
        scratch_shapes=[pltpu.VMEM((n, B), f32) for n in rows]
        + [pltpu.VMEM((ROWS, n // ROWS, B), f32) for n in rows]
        + [pltpu.VMEM((ROWS, n // ROWS, B), f32) for n in rows]
        + [pltpu.VMEM((STRIPS, gather_rows(q), B), f32) for q in range(nq)]
        + [
            pltpu.VMEM((M, M), bf16),
            pltpu.VMEM((M, M), bf16),
            pltpu.VMEM((2, 2 * B, M), bf16),
            pltpu.VMEM((B, M), f32),
            pltpu.VMEM((8, B), f32),
            pltpu.VMEM((1, M), f32),
            pltpu.SemaphoreType.DMA((nq * ROWS,)),
            pltpu.SemaphoreType.DMA((nq * ROWS,)),
            pltpu.SemaphoreType.DMA((nq * ROWS,)),
            pltpu.SemaphoreType.DMA((nq * ROWS,)),
            pltpu.SemaphoreType.DMA((nq * STRIPS * 2,)),
            pltpu.SemaphoreType.DMA((nq * STRIPS * 2,)),
            pltpu.SemaphoreType.DMA((ROWS,)),
            pltpu.SemaphoreType.DMA((ROWS,)),
            pltpu.VMEM(parent_blocks.shape, f32),
            pltpu.SMEM(shifts.shape, f32),
            pltpu.SMEM(orders.shape, jnp.int32),
            pltpu.SMEM(child_order.shape, jnp.int32),
            pltpu.SemaphoreType.DMA((4,)),
            pltpu.VMEM((EXTRA, B), f32),
            pltpu.VMEM((ROWS, EXTRA, B), f32),
            pltpu.SemaphoreType.DMA((STRIPS,)),
        ],
        compiler_params=pltpu.CompilerParams(
            collective_id=0, has_side_effects=True, vmem_limit_bytes=60 * 2**20
        ),
        cost_estimate=pl.CostEstimate(
            flops=8 * 3 * 2 * B * M * M, bytes_accessed=2 * 4 * B * M, transcendentals=0
        ),
        name="sign_steps",
    )(parent_blocks, shifts, orders, child_order)


def solution(mesh):
    in_specs = (P("row", "col", None), P(), P(), P())
    out_specs = P("row", "col", None)
    return jax.shard_map(local, mesh=mesh, in_specs=in_specs, out_specs=out_specs, check_vma=False)
```

```python
import jax
import jax.numpy as jnp
from jax import lax
from jax.experimental import pallas as pl
from jax.experimental.pallas import tpu as pltpu
from jax.sharding import PartitionSpec as P

MESH = pl.DeviceIdType.MESH
f32, bf16 = jnp.float32, jnp.bfloat16

SIDE = 4
STRIPS = SIDE * SIDE
ROWS = 8
B = 128
M = STRIPS * B
SPAN = M // SIDE

HALVES = ((0, 2), (2, 0), (2, 2))
CHUNKS = (
    ("x", ((0, 0), (0, 1))),
    ("z", ((2, 1),) + HALVES),
    ("x", ((1, 0), (1, 1))),
    ("z", ((1, 2), (1, 3))),
)
ORDER = (
    ("fill", 0), ("spread", 0), ("fill", 1), ("spread", 1), ("fill", 2), ("extra", 0), ("spread", 2), ("choose", 0),
    ("choose", 1), ("fill", 3), ("spread", 3), ("take", 0), ("begin", 0), ("choose", 2), ("begin", 1), ("lineA", 0),
    ("begin", 2), ("lineB", 0), ("choose", 3), ("lineB", 1), ("lineA", 1), ("begin", 3), ("near", 0, 0, 1),
    ("lineA", 2), ("near", 1, -1, 1), ("near", 1, -1, -1), ("line_end", 1), ("lineB", 3), ("lineA", 3),
    ("unpack", 1, 0), ("line_end", 0), ("near", 0, 0, -1), ("near", 1, 0, -1), ("lineB", 2), ("near", 1, 2, 1),
    ("near", 0, 1, -1), ("line_end", 3), ("near", 1, 1, -1), ("near", 1, 1, 1), ("near", 1, 0, 1), ("near", 1, 2, -1),
    ("near", 0, 2, -1), ("unpack", 1, 1), ("near", 0, -1, 1), ("near", 3, 0, 1), ("near", 0, 1, 1), ("unpack", 0, 0),
    ("near", 0, 2, 1), ("near", 3, 0, -1), ("near", 0, -1, -1), ("line_end", 2), ("unpack", 3, 0),
    ("near", 3, -1, -1), ("near", 2, -1, -1), ("near", 2, 0, 1), ("unpack", 1, 3), ("unpack", 2, 0),
    ("near", 2, -1, 1), ("unpack", 0, 3), ("near", 3, -1, 1), ("near", 2, 1, 1), ("near", 2, 0, -1),
    ("near", 3, 1, 1), ("unpack", 0, 1), ("halves", 1), ("near", 3, 2, 1), ("near", 2, 1, -1), ("near", 3, 2, -1),
    ("unpack", 3, 1), ("near", 3, 1, -1), ("far", 0), ("near", 2, 2, -1), ("unpack", 0, 2), ("near", 2, 2, 1),
    ("unpack", 2, 3), ("far", 1), ("unpack", 1, 2), ("unpack", 3, 3), ("halves", 2), ("unpack", 2, 1), ("far", 2),
    ("unpack", 2, 2), ("far", 3), ("unpack", 3, 2),
)
LINE = {"x": (0, 1), "z": (1, 0)}


DIAGONAL = (0, 0)
EXTRA = 8


def block_rows(d):
    return B // 2 if d in HALVES or d == DIAGONAL else B


def chunk_rows(q):
    return sum(block_rows(d) for d in CHUNKS[q][1])


def gather_rows(q):
    return chunk_rows(q) + (EXTRA if DIAGONAL in CHUNKS[q][1] else 0)


def offset(q, d):
    total = 0
    for e in CHUNKS[q][1]:
        if e == d:
            return total
        total += block_rows(e)


def plus(r, e, k=1):
    return ((r[0] + k * e[0]) % SIDE, (r[1] + k * e[1]) % SIDE)


def flat(r):
    return SIDE * r[0] + r[1]


def split(v):
    high = v.astype(bf16)
    return high, (v - high.astype(f32)).astype(bf16)


def kernel(x_hbm, shifts_hbm, orders_hbm, child_hbm, o_hbm, *scratch):
    nq = len(CHUNKS)
    pack, parts, chosen, stage = (scratch[i * nq : (i + 1) * nq] for i in range(4))
    sh, sl, lhs, strip, ssq, scale, s1, r1, s2, r2, s3, r3, s4, r4 = scratch[4 * nq : 4 * nq + 14]
    x_ref, shifts, orders, child, arg_sems, extra_out, extra_in, out_sems = scratch[4 * nq + 14 :]

    fetches = [
        pltpu.make_async_copy(src, dst, arg_sems.at[i])
        for i, (src, dst) in enumerate(
            ((x_hbm, x_ref), (shifts_hbm, shifts), (orders_hbm, orders), (child_hbm, child))
        )
    ]
    for fetch in fetches:
        fetch.start()

    row, col = lax.axis_index("row"), lax.axis_index("col")
    turned = lax.rem(row, 2)
    step_z, step_x = SIDE - (SIDE - 1) * turned, 1 + (SIDE - 1) * turned
    z, x = lax.rem(col // step_z, SIDE), lax.rem(col // step_x, SIDE)
    true_z, true_x = col // SIDE, lax.rem(col, SIDE)

    def place(r):
        return lax.rem(z + r[0], SIDE) * step_z + lax.rem(x + r[1], SIDE) * step_x

    def to_row(delta):
        return {"row": lax.rem(row + delta, ROWS)}

    def to_col(e, sign):
        return {"col": place((e[0] * (1 if sign > 0 else SIDE - 1), e[1] * (1 if sign > 0 else SIDE - 1)))}

    barrier = pltpu.get_barrier_semaphore()
    for delta in range(1, ROWS):
        pl.semaphore_signal(barrier, inc=1, device_id=to_row(delta), device_id_type=MESH)
    for e in LINE.values():
        for sign in (1, -1):
            pl.semaphore_signal(barrier, inc=1, device_id=to_col(e, sign), device_id_type=MESH)

    for fetch in fetches:
        fetch.wait()

    order, shift = orders[row], shifts[row]
    eye = (
        lax.broadcasted_iota(jnp.int32, (B, B), 0) == lax.broadcasted_iota(jnp.int32, (B, B), 1)
    )

    half_row = lax.broadcasted_iota(jnp.int32, (B // 2, B), 0)
    half_lane = lax.broadcasted_iota(jnp.int32, (B // 2, B), 1)
    upper = half_row <= half_lane
    lower_eye = half_lane == half_row + B // 2

    def fill(q):
        for d in CHUNKS[q][1]:
            there = lax.rem(true_z + d[0], SIDE) * SIDE + lax.rem(true_x + d[1], SIDE)
            blk = x_ref[0, :, pl.ds(pl.multiple_of(there * B, B), B)]
            if d == DIAGONAL:
                blk = blk - jnp.where(eye, shift, jnp.float32(0.0))
            live = jnp.maximum(col, there) * B < order
            blk = blk * jnp.where(live, jnp.float32(1.0), jnp.float32(0.0))
            at = offset(q, d)
            if d in HALVES:
                leads = (true_x if d[0] == 0 else true_z) < SIDE // 2
                one = jnp.where(leads, jnp.float32(1.0), jnp.float32(0.0))
                mirror = blk.T
                pack[q][at : at + B // 2] = blk[: B // 2] * one + mirror[B // 2 :] * (1.0 - one)
            elif d == DIAGONAL:
                top, bottom = blk[: B // 2], blk[B // 2 :]
                pack[q][at : at + B // 2] = jnp.where(upper, top, pltpu.roll(bottom, B // 2, 1))
                last = jnp.sum(jnp.where(lower_eye, bottom, 0.0), axis=0, keepdims=True)
                extra_out[...] = jnp.broadcast_to(last, (EXTRA, B))
            else:
                pack[q][at : at + B] = blk

    first, second = {}, {}

    def spread(q):
        n = chunk_rows(q) // ROWS
        for delta in range(1, ROWS):
            j = lax.rem(row + delta, ROWS)
            copy = pltpu.make_async_remote_copy(
                src_ref=pack[q].at[pl.ds(pl.multiple_of(j * n, 8), n)],
                dst_ref=parts[q].at[row],
                send_sem=s1.at[q * ROWS + delta],
                recv_sem=r1.at[q * ROWS + delta],
                device_id=to_row(delta),
                device_id_type=MESH,
            )
            copy.start()
            first[q, delta] = copy
        parts[q][row] = pack[q][pl.ds(pl.multiple_of(row * n, 8), n)]

    def choose(q):
        n = chunk_rows(q) // ROWS
        for delta in range(1, ROWS):
            first[q, delta].wait_recv()
        mine = pl.ds(pl.multiple_of(row * n, 8), n)
        for delta in range(1, ROWS):
            k = lax.rem(row + delta, ROWS)
            chosen[q][delta] = parts[q][child[k]]
            copy = pltpu.make_async_remote_copy(
                src_ref=chosen[q].at[delta],
                dst_ref=stage[q].at[0, mine],
                send_sem=s2.at[q * ROWS + delta],
                recv_sem=r2.at[q * ROWS + delta],
                device_id=to_row(delta),
                device_id_type=MESH,
            )
            copy.start()
            second[q, delta] = copy
        stage[q][0, mine] = parts[q][child[row]]

    fourth = {}

    def extra():
        for delta in range(1, ROWS):
            copy = pltpu.make_async_remote_copy(
                src_ref=extra_out,
                dst_ref=extra_in.at[row],
                send_sem=s4.at[delta],
                recv_sem=r4.at[delta],
                device_id=to_row(delta),
                device_id_type=MESH,
            )
            copy.start()
            fourth[delta] = copy
        extra_in[row] = extra_out[...]

    def take():
        for delta in range(1, ROWS):
            fourth[delta].wait_recv()
        stage[0][0, chunk_rows(0) :] = extra_in[child[row]]

    third = {}

    def send(q, r, half, e, sign):
        n = gather_rows(q)
        cut = (n // 2 + 7) // 8 * 8
        rows = {"all": pl.ds(0, n), "top": pl.ds(0, cut), "low": pl.ds(cut, n - cut)}[half]
        lands = plus(r, e, -sign)
        slot = (q * STRIPS + flat(lands)) * 2 + (1 if half == "low" else 0)
        copy = pltpu.make_async_remote_copy(
            src_ref=stage[q].at[flat(r), rows],
            dst_ref=stage[q].at[flat(lands), rows],
            send_sem=s3.at[slot],
            recv_sem=r3.at[slot],
            device_id=to_col(e, sign),
            device_id_type=MESH,
        )
        copy.start()
        third[q, lands, half] = copy

    def wait(q, r, half):
        third[q, r, half].wait_recv()

    def axes(q):
        a = LINE[CHUNKS[q][0]]
        return a, (a[1], a[0])

    def across(q, r):
        _, b = axes(q)
        send(q, r, "all", b, 1)
        send(q, r, "all", b, -1)

    def begin_gather(q):
        a, b = axes(q)
        for delta in range(1, ROWS):
            second[q, delta].wait_recv()
        send(q, (0, 0), "all", a, 1)
        send(q, (0, 0), "all", a, -1)
        across(q, (0, 0))

    ssq[...] = jnp.zeros_like(ssq)

    def put(i, j, blk):
        at_i, at_j = pl.ds(pl.multiple_of(i * B, B), B), pl.ds(pl.multiple_of(j * B, B), B)
        high, low = split(blk)
        sh[at_i, at_j] = high
        sl[at_i, at_j] = low
        if i is not j:
            high, low = split(blk.T)
            sh[at_j, at_i] = high
            sl[at_j, at_i] = low

    def square(blk, weight):
        ssq[...] += weight * jnp.sum((blk * blk).reshape(-1, 8, B), axis=0)

    def diagonal(part, last):
        mirror = jnp.concatenate([part, jnp.zeros_like(part)], axis=0).T
        above = mirror[: B // 2]
        top = jnp.where(upper, part, above)
        right = jnp.where(
            half_lane < half_row + B // 2, pltpu.roll(part, B // 2, 1), pltpu.roll(above, B // 2, 1)
        )
        right = jnp.where(lower_eye, last, right)
        bottom = jnp.where(half_lane < B // 2, mirror[B // 2 :], right)
        return jnp.concatenate([top, bottom], axis=0)

    def unpack(q, k):
        if all(d in HALVES for d in CHUNKS[q][1]):
            return
        a, b = axes(q)

        def body(t, _):
            rz, rx = t * a[0] + k * b[0], t * a[1] + k * b[1]
            r = rz * SIDE + rx
            for d in CHUNKS[q][1]:
                if d in HALVES:
                    continue
                at = offset(q, d)
                if d == DIAGONAL:
                    blk = diagonal(stage[q][r, at : at + B // 2], stage[q][r, chunk_rows(q) :][0:1])
                    square(blk, 1.0)
                    put(r, r, blk)
                else:
                    blk = stage[q][r, at : at + B]
                    square(blk, 2.0)
                    dz, dx = d[0] + (d[1] - d[0]) * turned, d[1] + (d[0] - d[1]) * turned
                    put(r, lax.rem(rz + dz, SIDE) * SIDE + lax.rem(rx + dx, SIDE), blk)
            return 0

        lax.fori_loop(0, SIDE, body, 0)

    def unpack_halves(q, early):
        pairs = {
            (0, 2): ((4, 1, 1, 1),) if early else ((4, 1, 1, 0),),
            (2, 0): ((4, 2, 1, 0), (2, 1, 1, 3)) if early else ((2, 1, 1, 2),),
            (2, 2): ((4, 2, 2, 1),) if early else ((4, 2, 2, 0),),
        }
        for d in HALVES:
            at = offset(q, d) + (offset(q, d[::-1]) - offset(q, d)) * turned
            half = pl.ds(pl.multiple_of(at, B // 2), B // 2)
            for count, per, step, start in pairs[d]:

                def body(t, _):
                    rz, rx = t // per, lax.rem(t, per) * step + start
                    if d[0] == 0:
                        leads = lax.rem(x + rx, SIDE) < SIDE // 2
                    elif d[1] == 0:
                        leads = lax.rem(z + rz, SIDE) < SIDE // 2
                    else:
                        leads = lax.rem(z + rz + (x + rx - z - rz) * turned, SIDE) < SIDE // 2
                    r = rz * SIDE + rx
                    o = lax.rem(rz + d[0], SIDE) * SIDE + lax.rem(rx + d[1], SIDE)
                    lead = jnp.where(leads, r, o)
                    trail = r + o - lead
                    blk = jnp.concatenate(
                        [stage[q][lead, half], stage[q][trail, half]], axis=0
                    )
                    square(blk, 2.0)
                    put(lead, trail, blk)
                    return 0

                lax.fori_loop(0, count, body, 0)

    def line_a(q):
        a, b = axes(q)
        wait(q, plus((0, 0), a, -1), "all")
        send(q, plus((0, 0), a, -1), "top", a, 1)
        across(q, plus((0, 0), a, -1))

    def line_b(q):
        a, b = axes(q)
        wait(q, a, "all")
        send(q, a, "low", a, -1)
        across(q, a)

    def line_end(q):
        a, b = axes(q)
        far = plus((0, 0), a, 2)
        wait(q, far, "top")
        wait(q, far, "low")
        across(q, far)

    def near(q, k, side):
        a, b = axes(q)
        r = plus(plus((0, 0), a, k), b, side)
        wait(q, r, "all")
        send(q, r, "top" if side < 0 else "low", b, -side)

    def far(q):
        a, b = axes(q)
        for k in (0, -1, 1, 2):
            r = plus(plus((0, 0), a, k), b, 2)
            wait(q, r, "top")
            wait(q, r, "low")

    steps = {
        "fill": fill,
        "spread": spread,
        "choose": choose,
        "extra": lambda _: extra(),
        "take": lambda _: take(),
        "begin": begin_gather,
        "lineA": line_a,
        "lineB": line_b,
        "line_end": line_end,
        "near": near,
        "far": far,
        "unpack": unpack,
        "halves": lambda i: unpack_halves(1, i == 1),
    }
    entered = False
    for name, *args in ORDER:
        if name == "spread" and not entered:
            pl.semaphore_wait(barrier, ROWS - 1 + 4)
            entered = True
        steps[name](*args)

    order_here = orders[child[row]]
    root = jnp.sqrt(jnp.full((1, M), order_here, jnp.int32).astype(f32))
    total = jnp.sum(jnp.sum(ssq[...], axis=0, keepdims=True), axis=1, keepdims=True)
    scale[...] = root / (2.0 * jnp.sqrt(jnp.broadcast_to(total, (1, M)) + 1e-06))

    def load(k, v, cs=slice(None)):
        high, low = split(v)
        lhs[k, 0:B, cs] = high
        lhs[k, B : 2 * B, cs] = low

    def quarter(k, cs):
        both = jnp.dot(lhs[k], sh[:, cs], preferred_element_type=f32)
        low = jnp.dot(lhs[k, 0:B], sl[:, cs], preferred_element_type=f32)
        return (both[0:B] + both[B : 2 * B] + low) * scale[:, cs]

    spans = [pl.ds(j * SPAN, SPAN) for j in range(SIDE)]

    for cs in spans:
        own = (sh[0:B, cs].astype(f32) + sl[0:B, cs].astype(f32)) * scale[:, cs]
        strip[:, cs] = own
        load(0, own, cs)

    for cs in spans:
        load(1, quarter(0, cs), cs)
    for cs in spans:
        v = 1.5 * strip[:, cs] - 0.5 * quarter(1, cs)
        strip[:, cs] = v
        load(0, -0.125 * v, cs)

    def horner(m, _):
        weight = jnp.where(m == 0, jnp.float32(0.75), jnp.float32(-1.125))
        for cs in spans:
            load(1, quarter(0, cs), cs)
        for cs in spans:
            load(0, quarter(1, cs) + weight * strip[:, cs], cs)
        return 0

    lax.fori_loop(0, 2, horner, 0)

    for cs in spans:
        load(1, quarter(0, cs), cs)
    leaving = []
    for j, cs in enumerate(spans):
        strip[:, cs] = (quarter(1, cs) + 1.5 * strip[:, cs]) * root[:, 0:SPAN]
        for rx in range(SIDE):
            r = flat((j, rx))
            copy = pltpu.make_async_copy(
                strip.at[:, pl.ds(r * B, B)],
                o_hbm.at[0, :, pl.ds(pl.multiple_of(place((j, rx)) * B, B), B)],
                out_sems.at[r],
            )
            copy.start()
            leaving.append(copy)
    for copy in leaving:
        copy.wait()

    for copies in (first, second, third, fourth):
        for copy in copies.values():
            copy.wait_send()


def local(parent_blocks, shifts, orders, child_order):
    nq = len(CHUNKS)
    rows = [chunk_rows(q) for q in range(nq)]
    anywhere = pl.BlockSpec(memory_space=pl.ANY)
    return pl.pallas_call(
        kernel,
        out_shape=jax.ShapeDtypeStruct(parent_blocks.shape, f32),
        in_specs=[anywhere] * 4,
        out_specs=anywhere,
        scratch_shapes=[pltpu.VMEM((n, B), f32) for n in rows]
        + [pltpu.VMEM((ROWS, n // ROWS, B), f32) for n in rows]
        + [pltpu.VMEM((ROWS, n // ROWS, B), f32) for n in rows]
        + [pltpu.VMEM((STRIPS, gather_rows(q), B), f32) for q in range(nq)]
        + [
            pltpu.VMEM((M, M), bf16),
            pltpu.VMEM((M, M), bf16),
            pltpu.VMEM((2, 2 * B, M), bf16),
            pltpu.VMEM((B, M), f32),
            pltpu.VMEM((8, B), f32),
            pltpu.VMEM((1, M), f32),
            pltpu.SemaphoreType.DMA((nq * ROWS,)),
            pltpu.SemaphoreType.DMA((nq * ROWS,)),
            pltpu.SemaphoreType.DMA((nq * ROWS,)),
            pltpu.SemaphoreType.DMA((nq * ROWS,)),
            pltpu.SemaphoreType.DMA((nq * STRIPS * 2,)),
            pltpu.SemaphoreType.DMA((nq * STRIPS * 2,)),
            pltpu.SemaphoreType.DMA((ROWS,)),
            pltpu.SemaphoreType.DMA((ROWS,)),
            pltpu.VMEM(parent_blocks.shape, f32),
            pltpu.SMEM(shifts.shape, f32),
            pltpu.SMEM(orders.shape, jnp.int32),
            pltpu.SMEM(child_order.shape, jnp.int32),
            pltpu.SemaphoreType.DMA((4,)),
            pltpu.VMEM((EXTRA, B), f32),
            pltpu.VMEM((ROWS, EXTRA, B), f32),
            pltpu.SemaphoreType.DMA((STRIPS,)),
        ],
        compiler_params=pltpu.CompilerParams(
            collective_id=0, has_side_effects=True, vmem_limit_bytes=60 * 2**20
        ),
        cost_estimate=pl.CostEstimate(
            flops=8 * 3 * 2 * B * M * M, bytes_accessed=2 * 4 * B * M, transcendentals=0
        ),
        name="sign_steps",
    )(parent_blocks, shifts, orders, child_order)


def solution(mesh):
    in_specs = (P("row", "col", None), P(), P(), P())
    out_specs = P("row", "col", None)
    return jax.shard_map(local, mesh=mesh, in_specs=in_specs, out_specs=out_specs, check_vma=False)
```
